256 devices in a mesh: row: 16 (over x_lo, y, core), col: 8 (over z), rep: 2 (over x_hi).
Axes of the slice: x: 4 (x_hi: 2, x_lo: 2; x = x_hi * 2 + x_lo), y: 4, z: 8, core: 2. Of those that a mesh axis runs over, the one named last changes fastest.
Arguments:
- pair: bfloat16 [1024, 512, 128], P(('rep', 'row'), 'col'), parts along dimension 0, may hold values from -6 to 6
- pad_mask: int32 [1024], P('rep'), parts along dimension 0, may hold values 0 or 1
- crop_mask: int32 [1024], P('rep'), parts along dimension 0, may hold values 0 or 1
- left_proj: bfloat16 [128, 128], replicated, may hold values from -0.5 to 0.5
- left_gate: bfloat16 [128, 128], replicated, may hold values from -0.5 to 0.5
- right_proj: bfloat16 [128, 128], replicated, may hold values from -0.5 to 0.5
- right_gate: bfloat16 [128, 128], replicated, may hold values from -0.5 to 0.5
- out_gate: bfloat16 [128, 128], replicated, may hold values from -0.5 to 0.5
- out_proj: bfloat16 [128, 128], replicated, may hold values from -0.5 to 0.5
- cotangent: bfloat16 [1024, 512, 128], P(('rep', 'row'), 'col'), parts along dimension 0, may hold values from -6 to 6
Outputs:
- result: bfloat16 [1024, 512, 128], P(('rep', 'row'), 'col'), parts along dimension 0
- grad_pair: bfloat16 [1024, 512, 128], P(('rep', 'row'), 'col'), parts along dimension 0
- weight_grads: float32 [12, 128, 128], P('rep'), parts along dimension 0
The draws below stay inside these ranges and needn't reach their ends.
There are 2 independent parts, one for each index of `rep`. The reference program is written for one: setup_inputs(seed, part) draws one part's arguments, and reference() takes and returns one part's arrays. A program takes and returns all parts, laid end to end along the dimension named above; an argument that names none is the same for every part. Nothing has to cross between parts.
Inputs may be any that keep to these rules, and one draw needn't show every extreme that they name: pad_mask and crop_mask hold only 0 and 1.
All inputs are finite; a program needn't handle non-finite values.
Results may differ from the reference program's by a relative error of at most 0.025.
Values may be sent and summed in bfloat16 or wider, within the bound.
A program may use at most 128 MiB of HBM per device.

```python
import jax
import jax.numpy as jnp
from jax import lax

C = 128
TOK_ROW = 32
TOKENS = 512
TOK_COL = 64
N_ROW = 16
N_COL = 8


def touch_ends(values, stream_key, least, top_value):
    index_at = [jax.random.randint(jax.random.fold_in(stream_key, axis), (), 0, length) for axis, length in enumerate(values.shape)]
    main_axis = values.shape.index(max(values.shape))
    next_to = index_at[:main_axis] + [(index_at[main_axis] + 1) % values.shape[main_axis]] + index_at[main_axis + 1:]
    return values.at[tuple(index_at)].set(least).at[tuple(next_to)].set(top_value)


def shard_levels(rng, dims, shards, low, largest):
    loudness, own = 1.0, jax.random.fold_in(rng, 6)
    for position, parts in shards:
        draws = jnp.exp(jax.random.uniform(jax.random.fold_in(own, position), (parts,), jnp.float32, low / len(shards), largest / len(shards)))
        loudness = loudness * jnp.repeat(draws, dims[position] // parts).reshape([-1 if axis == position else 1 for axis in range(len(dims))])
    return loudness


def normal_values(key, extent, scale, limit, shards=(), held_as=jnp.bfloat16):
    loudness = shard_levels(key, extent, shards, -0.22, 0.18) if shards else 1.0
    drawn = jax.random.normal(key, extent, jnp.float32) * scale * loudness
    return jnp.minimum(jnp.maximum(drawn, -limit), limit).astype(held_as)


def setup_inputs(seed: int = 0, part: int = 0) -> dict:
    key_of = jax.random.split(jax.random.key(seed), 11)
    own_keys = jax.random.split(jax.random.fold_in(key_of[10], part), 11)
    pair = normal_values(own_keys[0], (TOKENS, TOKENS, C), 1.0, 6.0, ((0, 16), (1, 8)))
    pad_mask = touch_ends((jax.random.randint(own_keys[1], (TOKENS,), 0, 8) < 7).astype(jnp.int32), jax.random.fold_in(own_keys[1], 1), 0, 1)
    crop_mask = touch_ends((jax.random.randint(own_keys[2], (TOKENS,), 0, 4) < 3).astype(jnp.int32), jax.random.fold_in(own_keys[2], 1), 0, 1)
    left_proj = normal_values(key_of[3], (C, C), C ** -0.5, 0.5)
    left_gate = normal_values(key_of[4], (C, C), C ** -0.5, 0.5)
    right_proj = normal_values(key_of[5], (C, C), C ** -0.5, 0.5)
    right_gate = normal_values(key_of[6], (C, C), C ** -0.5, 0.5)
    out_gate = normal_values(key_of[7], (C, C), C ** -0.5, 0.5)
    out_proj = normal_values(key_of[8], (C, C), C ** -0.5, 0.5)
    cotangent = normal_values(own_keys[9], (TOKENS, TOKENS, C), 1.0, 6.0, ((0, 16), (1, 8)))
    return dict(pair=pair, pad_mask=pad_mask, crop_mask=crop_mask, left_proj=left_proj, left_gate=left_gate, right_proj=right_proj, right_gate=right_gate, out_gate=out_gate, out_proj=out_proj, cotangent=cotangent)


def layer_norm(values):
    center = values - lax.optimization_barrier(jnp.mean(values, -1, keepdims=True))
    spread = lax.optimization_barrier(jnp.mean(center * center, -1, keepdims=True))
    return center * lax.rsqrt(spread + 1e-05)

def project(source, weight):
    return jnp.einsum('ijc,cd->ijd', source.astype(jnp.float32), weight.astype(jnp.float32))

def back_project(source, weight):
    return jnp.einsum('ijd,cd->ijc', source.astype(jnp.float32), weight.astype(jnp.float32))

def outer_sum(left, right):
    return jnp.einsum('ijc,ijd->cd', left.astype(jnp.float32), right.astype(jnp.float32))

def rounded(values):
    return lax.optimization_barrier(values.astype(jnp.bfloat16)).astype(jnp.float32)

def reference(pair, pad_mask, crop_mask, left_proj, left_gate, right_proj, right_gate, out_gate, out_proj, cotangent):
    pad_float = pad_mask.astype(jnp.float32)
    crop_float = crop_mask.astype(jnp.float32)
    pair_mask = (pad_float[:, None] * pad_float[None, :])[:, :, None]
    crop_pair = (crop_float[:, None] * crop_float[None, :])[:, :, None]
    pair_float = pair.astype(jnp.float32)
    normed = layer_norm(pair_float).astype(jnp.bfloat16)
    left_value = project(normed, left_proj)
    left_sig = jax.nn.sigmoid(project(normed, left_gate))
    right_value = project(normed, right_proj)
    right_sig = jax.nn.sigmoid(project(normed, right_gate))
    gate_value = jax.nn.sigmoid(project(normed, out_gate))
    left_edge = (pair_mask * left_sig * left_value).astype(jnp.bfloat16)
    right_edge = (pair_mask * right_sig * right_value).astype(jnp.bfloat16)
    left_wide = left_edge.astype(jnp.float32)
    right_wide = right_edge.astype(jnp.float32)
    summed = jnp.zeros(pair.shape, jnp.float32)
    for block in range(N_COL):
        lower = block * TOK_COL
        partial_sum = jnp.einsum('ikc,jkc->ijc', left_wide[:, lower:lower + TOK_COL], right_wide[:, lower:lower + TOK_COL])
        summed = summed + rounded(partial_sum)
    normed_sum = layer_norm(summed).astype(jnp.bfloat16)
    projected = project(normed_sum, out_proj)
    result = (crop_pair * gate_value * projected).astype(jnp.bfloat16)
    upstream = crop_pair * cotangent.astype(jnp.float32)
    grad_projected = (upstream * gate_value).astype(jnp.bfloat16)
    grad_gate_logit = (upstream * projected * gate_value * (1.0 - gate_value)).astype(jnp.bfloat16)
    grad_normed_sum = back_project(grad_projected, out_proj)
    _, sum_pullback = jax.vjp(layer_norm, summed)
    grad_summed = sum_pullback(grad_normed_sum)[0].astype(jnp.bfloat16)
    grad_wide = grad_summed.astype(jnp.float32)
    grad_left = jnp.einsum('ijc,jkc->ikc', grad_wide, right_wide)
    grad_right = jnp.zeros(pair.shape, jnp.float32)
    for block in range(N_ROW):
        lower = block * TOK_ROW
        term = jnp.einsum('ijc,ikc->jkc', grad_wide[lower:lower + TOK_ROW], left_wide[lower:lower + TOK_ROW])
        grad_right = grad_right + rounded(term)
    grad_left_value = (grad_left * pair_mask * left_sig).astype(jnp.bfloat16)
    grad_left_logit = (grad_left * pair_mask * left_value * left_sig * (1.0 - left_sig)).astype(jnp.bfloat16)
    grad_right_value = (grad_right * pair_mask * right_sig).astype(jnp.bfloat16)
    grad_right_logit = (grad_right * pair_mask * right_value * right_sig * (1.0 - right_sig)).astype(jnp.bfloat16)
    grad_normed = back_project(grad_left_value, left_proj) + back_project(grad_left_logit, left_gate)
    grad_normed = grad_normed + back_project(grad_right_value, right_proj) + back_project(grad_right_logit, right_gate)
    grad_normed = grad_normed + back_project(grad_gate_logit, out_gate)
    _, pair_pullback = jax.vjp(layer_norm, pair_float)
    grad_pair = pair_pullback(grad_normed)[0].astype(jnp.bfloat16)
    weight_grads = jnp.stack([outer_sum(normed, grad_left_value), outer_sum(normed, grad_left_logit), outer_sum(normed, grad_right_value), outer_sum(normed, grad_right_logit), outer_sum(normed, grad_gate_logit), outer_sum(normed_sum, grad_projected)]) / jnp.float32(TOKENS)
    return (result, grad_pair, weight_grads)
```

```python
import jax
import jax.numpy as jnp
from jax import lax
from jax.experimental import pallas as pl
from jax.experimental.pallas import tpu as pltpu
from jax.sharding import PartitionSpec as P

MESH = pl.DeviceIdType.MESH


def for_peers(rows, cols, act):
    row, col = lax.axis_index("row"), lax.axis_index("col")
    order = sorted(range(cols), key=lambda step: min(step, cols - step))

    def step(shift, carry):
        for hop in order:

            @pl.when(jnp.logical_or(shift > 0, hop > 0))
            def _():
                act(lax.rem(row + shift, rows), lax.rem(col + hop, cols))

        return carry

    lax.fori_loop(0, rows, step, 0)


def wait_bytes(ref, sem):
    pltpu.make_async_copy(ref, ref, sem).wait()


def sum_kernel(rows, cols, parts_ref, out_ref, held, total, sems):
    me = lax.axis_index("row") * cols + lax.axis_index("col")
    others = rows * cols - 1
    barrier = pltpu.get_barrier_semaphore()

    def greet(row, col):
        pl.semaphore_signal(
            barrier, inc=1, device_id={"row": row, "col": col}, device_id_type=MESH
        )

    for_peers(rows, cols, greet)
    pl.semaphore_wait(barrier, others)

    def scatter(row, col):
        pltpu.make_async_remote_copy(
            src_ref=parts_ref.at[row * cols + col],
            dst_ref=held.at[me],
            send_sem=sems.at[0],
            recv_sem=sems.at[1],
            device_id={"row": row, "col": col},
            device_id_type=MESH,
        ).start()

    for_peers(rows, cols, scatter)
    held[me] = parts_ref[me]
    wait_bytes(held.at[pl.ds(0, others)], sems.at[1])
    total[...] = jnp.sum(held[...], axis=0)
    out_ref[me] = total[...]

    def spread(row, col):
        pltpu.make_async_remote_copy(
            src_ref=total,
            dst_ref=out_ref.at[me],
            send_sem=sems.at[2],
            recv_sem=sems.at[3],
            device_id={"row": row, "col": col},
            device_id_type=MESH,
        ).start()

    for_peers(rows, cols, spread)
    wait_bytes(held.at[pl.ds(0, others)], sems.at[0])
    wait_bytes(held.at[pl.ds(0, others)], sems.at[2])
    wait_bytes(held.at[pl.ds(0, others)], sems.at[3])


def sum_over_part(values):
    rows, cols = lax.axis_size("row"), lax.axis_size("col")
    count, height, width = values.shape
    devices = rows * cols
    share = height // devices
    parts = values.reshape(count, devices, share, width).transpose(1, 0, 2, 3)
    parts = parts.reshape(devices, count * share, width)
    out = pl.pallas_call(
        lambda *refs: sum_kernel(rows, cols, *refs),
        out_shape=jax.ShapeDtypeStruct(parts.shape, jnp.float32),
        in_specs=[pl.BlockSpec(memory_space=pltpu.VMEM)],
        out_specs=pl.BlockSpec(memory_space=pltpu.VMEM),
        scratch_shapes=[
            pltpu.VMEM(parts.shape, jnp.float32),
            pltpu.VMEM(parts.shape[1:], jnp.float32),
            pltpu.SemaphoreType.DMA((4,)),
        ],
        compiler_params=pltpu.CompilerParams(
            collective_id=1, has_side_effects=True, vmem_limit_bytes=32 * 2**20
        ),
        name="weight_sum",
    )(parts)
    out = out.reshape(devices, count, share, width).transpose(1, 0, 2, 3)
    return out.reshape(values.shape)


def layer_norm(values):
    center = values - jnp.mean(values, -1, keepdims=True)
    spread = jnp.mean(center * center, -1, keepdims=True)
    return center * lax.rsqrt(spread + 1e-05)


def project(source, weight):
    return jnp.einsum("ijc,cd->ijd", source, weight, preferred_element_type=jnp.float32)


def back_project(source, weight):
    return jnp.einsum("ijd,cd->ijc", source, weight, preferred_element_type=jnp.float32)


def outer_sum(left, right):
    return jnp.einsum("ijc,ijd->cd", left, right, preferred_element_type=jnp.float32)


def shards(
    pair,
    pad_mask,
    crop_mask,
    left_proj,
    left_gate,
    right_proj,
    right_gate,
    out_gate,
    out_proj,
    cotangent,
):
    row_count = pair.shape[0]
    col_count = pair.shape[1]
    row_devices = lax.axis_size("row")
    total = row_count * row_devices
    row_start = lax.axis_index("row") * row_count
    col_start = lax.axis_index("col") * col_count
    pad_float = pad_mask.astype(jnp.float32)
    crop_float = crop_mask.astype(jnp.float32)
    pad_rows = lax.dynamic_slice_in_dim(pad_float, row_start, row_count)
    pad_cols = lax.dynamic_slice_in_dim(pad_float, col_start, col_count)
    crop_rows = lax.dynamic_slice_in_dim(crop_float, row_start, row_count)
    crop_cols = lax.dynamic_slice_in_dim(crop_float, col_start, col_count)
    pair_mask = (pad_rows[:, None] * pad_cols[None, :])[:, :, None]
    crop_pair = (crop_rows[:, None] * crop_cols[None, :])[:, :, None]
    pair_float = pair.astype(jnp.float32)
    normed = layer_norm(pair_float).astype(jnp.bfloat16)
    left_value = project(normed, left_proj)
    left_sig = jax.nn.sigmoid(project(normed, left_gate))
    right_value = project(normed, right_proj)
    right_sig = jax.nn.sigmoid(project(normed, right_gate))
    left_edge = (pair_mask * left_sig * left_value).astype(jnp.bfloat16)
    right_edge = (pair_mask * right_sig * right_value).astype(jnp.bfloat16)
    right_panel = lax.all_gather(right_edge, "row", axis=0, tiled=True)
    gate_value = jax.nn.sigmoid(project(normed, out_gate))
    summed_cols = lax.psum_scatter(
        jnp.einsum(
            "jkc,ikc->jic", right_panel, left_edge, preferred_element_type=jnp.float32
        ).astype(jnp.bfloat16),
        "col",
        scatter_dimension=0,
        tiled=True,
    ).astype(jnp.float32)
    summed = jnp.transpose(summed_cols, (1, 0, 2))
    normed_sum = layer_norm(summed).astype(jnp.bfloat16)
    projected = project(normed_sum, out_proj)
    result = (crop_pair * gate_value * projected).astype(jnp.bfloat16)
    upstream = crop_pair * cotangent.astype(jnp.float32)
    grad_projected = (upstream * gate_value).astype(jnp.bfloat16)
    grad_gate_logit = (upstream * projected * gate_value * (1.0 - gate_value)).astype(jnp.bfloat16)
    grad_normed_sum = back_project(grad_projected, out_proj)
    _, sum_pullback = jax.vjp(layer_norm, summed)
    grad_summed = sum_pullback(grad_normed_sum)[0].astype(jnp.bfloat16)
    cotangent_panel = lax.all_gather(grad_summed, "col", axis=1, tiled=True)
    grad_left = jnp.einsum(
        "ijc,jkc->ikc", cotangent_panel, right_panel, preferred_element_type=jnp.float32
    )
    grad_right = lax.psum_scatter(
        jnp.einsum(
            "ijc,ikc->jkc", cotangent_panel, left_edge, preferred_element_type=jnp.float32
        ).astype(jnp.bfloat16),
        "row",
        scatter_dimension=0,
        tiled=True,
    ).astype(jnp.float32)
    grad_left_value = (grad_left * pair_mask * left_sig).astype(jnp.bfloat16)
    grad_left_logit = (grad_left * pair_mask * left_value * left_sig * (1.0 - left_sig)).astype(
        jnp.bfloat16
    )
    grad_right_value = (grad_right * pair_mask * right_sig).astype(jnp.bfloat16)
    grad_right_logit = (
        grad_right * pair_mask * right_value * right_sig * (1.0 - right_sig)
    ).astype(jnp.bfloat16)
    grad_normed = back_project(grad_left_value, left_proj) + back_project(
        grad_left_logit, left_gate
    )
    grad_normed = (
        grad_normed
        + back_project(grad_right_value, right_proj)
        + back_project(grad_right_logit, right_gate)
    )
    grad_normed = grad_normed + back_project(grad_gate_logit, out_gate)
    _, pair_pullback = jax.vjp(layer_norm, pair_float)
    grad_pair = pair_pullback(grad_normed)[0].astype(jnp.bfloat16)
    local_grads = jnp.stack(
        [
            outer_sum(normed, grad_left_value),
            outer_sum(normed, grad_left_logit),
            outer_sum(normed, grad_right_value),
            outer_sum(normed, grad_right_logit),
            outer_sum(normed, grad_gate_logit),
            outer_sum(normed_sum, grad_projected),
        ]
    ) / jnp.float32(total)
    weight_grads = sum_over_part(local_grads)
    return (result, grad_pair, weight_grads)


def solution(mesh):
    return jax.shard_map(
        shards,
        mesh=mesh,
        in_specs=(
            P(("rep", "row"), "col", None),
            P("rep"),
            P("rep"),
            P(),
            P(),
            P(),
            P(),
            P(),
            P(),
            P(("rep", "row"), "col", None),
        ),
        out_specs=(
            P(("rep", "row"), "col", None),
            P(("rep", "row"), "col", None),
            P("rep", None, None),
        ),
        check_vma=False,
    )
```

```python
import functools

import jax
import jax.numpy as jnp
from jax import lax
from jax.experimental import pallas as pl
from jax.experimental.pallas import tpu as pltpu
from jax.sharding import PartitionSpec as P

MESH = pl.DeviceIdType.MESH
F32 = jnp.float32
BF16 = jnp.bfloat16
EPS = 1e-05


def dot_nn(left, right):
    return jnp.dot(left, right, preferred_element_type=F32)


def dot_nt(left, right):
    return lax.dot_general(left, right, (((1,), (1,)), ((), ())), preferred_element_type=F32)


def dot_tn(left, right):
    return lax.dot_general(left, right, (((0,), (0,)), ((), ())), preferred_element_type=F32)


def mean_rows(values):
    return jnp.mean(values, axis=0, keepdims=True)


def wait_bytes(ref, sem):
    pltpu.make_async_copy(ref, ref, sem).wait()


def kernel(
    rows,
    cols,
    pair,
    cot,
    pad_row,
    crop_row,
    pad_col,
    crop_col,
    left_proj,
    left_gate,
    right_proj,
    right_gate,
    out_gate,
    out_proj,
    result,
    grad_pair,
    weight_grads,
    send_l,
    send_r,
    send_s,
    send_g,
    send_dl,
    send_dr,
    recv_l,
    recv_r,
    recv_s,
    recv_g,
    recv_dl,
    recv_dr,
    stage,
    spread,
    norm_t,
    xhat,
    scale,
    left_v,
    left_s,
    right_v,
    right_s,
    gate_c,
    gate_u,
    grad_ns,
    grad_n,
    norm_s,
    grad_p,
    grad_o,
    grad_e,
    w_left,
    w_right,
    w_out,
    w_proj,
    b_left,
    b_right,
    part_a,
    held_a,
    line_a,
    full_a,
    part_b,
    held_b,
    line_b,
    full_b,
    sems,
):
    row, col = lax.axis_index("row"), lax.axis_index("col")
    me = row * cols + col
    channels = rows * cols
    tiles, half_lanes = pair.shape[0] // 2, pair.shape[1]
    order = sorted(range(cols), key=lambda step: min(step, cols - step))
    barrier = pltpu.get_barrier_semaphore()

    def device(r, c):
        return {"row": r, "col": c}

    def for_rows(act, itself):
        def step(shift, carry):
            act(lax.rem(row + shift, rows))
            return carry

        lax.fori_loop(0 if itself else 1, rows, step, 0)

    def for_peers(act):
        def step(shift, carry):
            for hop in order[1:]:
                act(lax.rem(row + shift, rows), lax.rem(col + hop, cols))

            @pl.when(shift > 0)
            def _():
                act(lax.rem(row + shift, rows), col)

            return carry

        lax.fori_loop(0, rows, step, 0)

    def copy_to(src, dst, which, r, c):
        pltpu.make_async_remote_copy(
            src_ref=src,
            dst_ref=dst,
            send_sem=sems.at[2 * which],
            recv_sem=sems.at[2 * which + 1],
            device_id=device(r, c),
            device_id_type=MESH,
        ).start()

    def at_owner(ref, r, c):
        return ref.at[c, pl.ds(pl.multiple_of(r * tiles, tiles), tiles)]

    def to_owners(src, dst, which):
        dst[col, pl.ds(pl.multiple_of(row * tiles, tiles), tiles)] = src[me]
        for_peers(
            lambda r, c: copy_to(src.at[r * cols + c], at_owner(dst, row, col), which, r, c)
        )

    def from_owner(src, dst, which, r, c):
        copy_to(at_owner(src, r, c), dst.at[me], which, r, c)

    def arrived(which):
        wait_bytes(send_l.at[pl.ds(0, channels - 1)], sems.at[2 * which + 1])

    def sent(which):
        wait_bytes(send_l.at[pl.ds(0, channels - 1)], sems.at[2 * which])

    def for_tiles(body, unroll=2):
        def step(p, carry):
            body(p)
            return carry

        lax.fori_loop(0, tiles, step, 0, unroll=unroll)

    def lanes(p):
        return pl.ds(pl.multiple_of(p * 2 * half_lanes, 2 * half_lanes), 2 * half_lanes)

    def strided(p):
        return pl.ds(p, channels, stride=tiles)

    def pack(dst):
        dst[...] = stage[...].reshape(channels, tiles, 2 * half_lanes).astype(BF16)

    def unpack(src):
        stage[...] = src[...].astype(F32).reshape(channels * tiles, 2 * half_lanes)

    low = lax.broadcasted_iota(jnp.int32, (1, 2 * half_lanes), 1) < half_lanes

    def mask_of(row_ref, col_ref):
        line = col_ref[pl.ds(col, 1), :].astype(F32)
        line = jnp.concatenate([line, line], axis=1)

        def mask(p):
            first = row_ref[row * 2 * tiles + p].astype(F32)
            second = row_ref[row * 2 * tiles + tiles + p].astype(F32)
            return jnp.where(low, first, second) * line

        return mask

    pad, crop = mask_of(pad_row, pad_col), mask_of(crop_row, crop_col)

    def tile_t(ref, p):
        both = jnp.concatenate([ref[p], ref[p + tiles]], axis=0)
        return both.astype(F32).T

    def put_tile(ref, p, values):
        back = values.T.astype(BF16)
        ref[p] = back[:half_lanes]
        ref[p + tiles] = back[half_lanes:]

    for_peers(
        lambda r, c: pl.semaphore_signal(
            barrier, inc=1, device_id=device(r, c), device_id_type=MESH
        )
    )

    def flip(ref):
        return ref[...].astype(F32).T.astype(BF16)

    size = left_proj.shape[0]
    w_left[:size] = flip(left_proj)
    w_left[size:] = flip(left_gate)
    w_right[:size] = flip(right_proj)
    w_right[size:] = flip(right_gate)
    w_out[...] = flip(out_gate)
    w_proj[...] = flip(out_proj)
    b_left[:, :size] = left_proj[...]
    b_left[:, size:] = left_gate[...]
    b_right[:, :size] = right_proj[...]
    b_right[:, size:] = right_gate[...]

    def edge(p, normed, weight, value_ref, sig_ref):
        both = dot_nn(weight[...], normed)
        value, sig = both[:size], jax.nn.sigmoid(both[size:])
        value_ref[p] = value
        sig_ref[p] = sig
        stage[strided(p), :] = pad(p) * sig * value

    def left_tile(p):
        wide = tile_t(pair, p)
        center = wide - mean_rows(wide)
        rstd = lax.rsqrt(mean_rows(center * center) + EPS)
        hat = center * rstd
        xhat[p] = hat
        scale[p] = rstd
        normed = hat.astype(BF16)
        norm_t[:, lanes(p)] = normed
        edge(p, normed, w_left, left_v, left_s)

    for_tiles(left_tile)
    pack(send_l)
    pl.semaphore_wait(barrier, channels - 1)
    to_owners(send_l, recv_l, 0)
    for_tiles(lambda p: edge(p, norm_t[:, lanes(p)], w_right, right_v, right_s))
    pack(send_r)
    to_owners(send_r, recv_r, 1)

    def out_tile(p):
        gate = jax.nn.sigmoid(dot_nn(w_out[...], norm_t[:, lanes(p)]))
        upstream = crop(p) * tile_t(cot, p)
        projected_grad = (upstream * gate).astype(BF16)
        grad_p[:, lanes(p)] = projected_grad
        gate_c[p] = crop(p) * gate
        gate_u[p] = upstream * gate * (1.0 - gate)
        grad_ns[p] = dot_nn(out_proj[...], projected_grad)

    for_tiles(out_tile)

    width = 2 * half_lanes
    arrived(0)
    arrived(1)

    def spread_block(c, carry):
        raw = recv_r[c].astype(F32)
        turned = pltpu.roll(raw, half_lanes, 1)
        raw = raw.reshape(cols, rows // cols, tiles, width)
        turned = turned.reshape(cols, rows // cols, tiles, width)
        zero = jnp.zeros_like(raw)
        top = jnp.stack([jnp.where(low, raw, zero), jnp.where(low, turned, zero)], axis=2)
        bottom = jnp.stack([jnp.where(low, zero, turned), jnp.where(low, zero, raw)], axis=2)
        both = jnp.stack([top, bottom], axis=1)
        spread[:, lanes(c)] = both.reshape(cols * width, width).astype(BF16)
        return carry

    lax.fori_loop(0, cols, spread_block, 0)

    def whole(ref):
        return jnp.concatenate([ref[c] for c in range(cols)], axis=1)

    def send_column(src, dst, which, c, hop):
        for_rows(lambda r: from_owner(src, dst, which, r, c), hop != 0)

    def keep_own(src, dst):
        dst[me] = src[col, pl.ds(pl.multiple_of(row * tiles, tiles), tiles)]

    for hop in order[1:] + order[:1]:
        c = lax.rem(col + hop, cols)
        send_s[c] = dot_nt(whole(recv_l), spread[lanes(c), :]).astype(BF16)
        send_column(send_s, recv_s, 2, c, hop)
    keep_own(send_s, recv_s)

    arrived(2)
    unpack(recv_s)

    def sum_tile(p):
        sums = stage[strided(p), :]
        center = sums - mean_rows(sums)
        rstd = lax.rsqrt(mean_rows(center * center) + EPS)
        hat = center * rstd
        norm_s[:, lanes(p)] = hat.astype(BF16)
        grad = grad_ns[p]
        grad = rstd * (grad - mean_rows(grad) - hat * mean_rows(grad * hat))
        stage[strided(p), :] = grad

    for_tiles(sum_tile)
    pack(send_g)
    to_owners(send_g, recv_g, 3)

    def result_tile(p):
        projected = dot_nn(w_proj[...], norm_s[:, lanes(p)])
        put_tile(result, p, gate_c[p] * projected)
        logit = (gate_u[p] * projected).astype(BF16)
        grad_o[:, lanes(p)] = logit
        grad_n[p] = dot_nn(out_gate[...], logit)

    for_tiles(result_tile)
    inverse = 1.0 / (rows * 2 * tiles)

    def put_weight(ref, place, values):
        high = size // rows
        ref[:, place * high : (place + 1) * high, :] = (values * inverse).reshape(
            rows, high, size
        )

    put_weight(part_a, 2, dot_nt(norm_t[...], grad_o[...]))
    put_weight(part_a, 3, dot_nt(norm_s[...], grad_p[...]))

    arrived(3)
    for hop in order[1:] + order[:1]:
        c = lax.rem(col + hop, cols)
        send_dl[c] = dot_nn(whole(recv_g), spread[:, lanes(c)]).astype(BF16)
        send_column(send_dl, recv_dl, 4, c, hop)
    keep_own(send_dl, recv_dl)

    per = rows // cols

    def right_block(c, carry):
        outer = dot_tn(recv_g[c], whole(recv_l))
        for k in range(cols):
            part = outer[:, k * width : (k + 1) * width].reshape(2, per, 2, tiles, width)
            keep = jnp.where(low, part[0, :, 0], part[1, :, 1])
            turn = jnp.where(low, part[0, :, 1], part[1, :, 0])
            turn = pltpu.roll(turn.reshape(per * tiles, width), half_lanes, 1)
            at = pl.ds(pl.multiple_of(c * per * tiles, per * tiles), per * tiles)
            send_dr[k, at, :] = (keep.reshape(per * tiles, width) + turn).astype(BF16)
        return carry

    lax.fori_loop(0, cols, right_block, 0)
    for_peers(lambda r, c: from_owner(send_dr, recv_dr, 5, r, c))
    keep_own(send_dr, recv_dr)

    def weight_parts(part, held, which):
        held[row] = part[row]
        for_rows(lambda r: copy_to(part.at[r], held.at[row], which, r, col), False)

    def weight_lines(held, line, which):
        wait_bytes(held.at[pl.ds(0, rows - 1)], sems.at[2 * which + 1])
        line[col] = jnp.sum(held[...], axis=0)
        for hop in order[1:]:
            copy_to(line.at[col], line.at[col], which + 1, row, lax.rem(col + hop, cols))

    def weight_full(line, full, which):
        wait_bytes(line.at[pl.ds(0, cols - 1)], sems.at[2 * which + 3])
        full[row] = jnp.sum(line[...], axis=0)
        for_rows(lambda r: copy_to(full.at[row], full.at[row], which + 2, r, col), False)

    def weight_done(line, full, which, places):
        wait_bytes(full.at[pl.ds(0, rows - 1)], sems.at[2 * which + 5])
        high = size // rows
        for slot, place in enumerate(places):
            part = full[:, slot * high : (slot + 1) * high, :]
            weight_grads[place] = part.reshape(size, size)
        wait_bytes(full.at[pl.ds(0, rows - 1)], sems.at[2 * which])
        wait_bytes(line.at[pl.ds(0, cols - 1)], sems.at[2 * which + 2])
        wait_bytes(full.at[pl.ds(0, rows - 1)], sems.at[2 * which + 4])

    def edge_grads(p, value_ref, sig_ref):
        grad, sig = pad(p) * stage[strided(p), :], sig_ref[p]
        grad_v = grad * sig
        grad_e[:size, lanes(p)] = grad_v.astype(BF16)
        grad_e[size:, lanes(p)] = (grad_v * value_ref[p] * (1.0 - sig)).astype(BF16)

    arrived(4)
    unpack(recv_dl)

    def left_back(p):
        edge_grads(p, left_v, left_s)
        grad_n[p] += dot_nn(b_left[...], grad_e[:, lanes(p)])

    for_tiles(left_back)
    both = dot_nt(norm_t[...], grad_e[...])
    put_weight(part_a, 0, both[:, :size])
    put_weight(part_a, 1, both[:, size:])
    weight_parts(part_a, held_a, 6)
    weight_lines(held_a, line_a, 6)
    weight_full(line_a, full_a, 6)

    arrived(5)
    unpack(recv_dr)
    for_tiles(lambda p: edge_grads(p, right_v, right_s))
    both = dot_nt(norm_t[...], grad_e[...])
    put_weight(part_b, 0, both[:, :size])
    put_weight(part_b, 1, both[:, size:])
    weight_parts(part_b, held_b, 9)

    def pair_tile(p):
        grad = grad_n[p] + dot_nn(b_right[...], grad_e[:, lanes(p)])
        hat = xhat[p]
        grad = scale[p] * (grad - mean_rows(grad) - hat * mean_rows(grad * hat))
        put_tile(grad_pair, p, grad)

    for_tiles(pair_tile)
    weight_lines(held_b, line_b, 9)
    weight_full(line_b, full_b, 9)
    weight_done(line_a, full_a, 6, (0, 1, 4, 5))
    weight_done(line_b, full_b, 9, (2, 3))
    for which in range(6):
        sent(which)


def shards(
    pair,
    pad_mask,
    crop_mask,
    left_proj,
    left_gate,
    right_proj,
    right_gate,
    out_gate,
    out_proj,
    cotangent,
):
    rows, cols = lax.axis_size("row"), lax.axis_size("col")
    high, wide, size = pair.shape
    tiles, width, channels = high // 2, 2 * wide, rows * cols
    positions = tiles * width
    vmem = pl.BlockSpec(memory_space=pltpu.VMEM)
    smem = pl.BlockSpec(memory_space=pltpu.SMEM)
    at_home = pltpu.VMEM((channels, tiles, width), BF16)
    at_owner = pltpu.VMEM((cols, rows * tiles, width), BF16)
    wide_tiles = pltpu.VMEM((tiles, size, width), F32)
    flat = pltpu.VMEM((size, positions), BF16)
    pair_weights = pltpu.VMEM((2 * size, size), BF16)
    weight = pltpu.VMEM((size, size), BF16)
    back_weights = pltpu.VMEM((size, 2 * size), BF16)
    share = size // rows

    def sum_buffers(count):
        return [
            pltpu.VMEM((rows, count * share, size), F32),
            pltpu.VMEM((rows, count * share, size), F32),
            pltpu.VMEM((cols, count * share, size), F32),
            pltpu.VMEM((rows, count * share, size), F32),
        ]

    return pl.pallas_call(
        functools.partial(kernel, rows, cols),
        out_shape=(
            jax.ShapeDtypeStruct(pair.shape, BF16),
            jax.ShapeDtypeStruct(pair.shape, BF16),
            jax.ShapeDtypeStruct((6, size, size), F32),
        ),
        in_specs=[vmem, vmem, smem, smem] + [vmem] * 8,
        out_specs=(vmem, vmem, vmem),
        scratch_shapes=[
            at_home,
            at_home,
            at_owner,
            at_home,
            at_owner,
            at_owner,
            at_owner,
            at_owner,
            at_home,
            at_owner,
            at_home,
            at_home,
            pltpu.VMEM((channels * tiles, width), F32),
            pltpu.VMEM((cols * width, cols * width), BF16),
            flat,
            wide_tiles,
            pltpu.VMEM((tiles, 1, width), F32),
            wide_tiles,
            wide_tiles,
            wide_tiles,
            wide_tiles,
            wide_tiles,
            wide_tiles,
            wide_tiles,
            wide_tiles,
            flat,
            flat,
            flat,
            pltpu.VMEM((2 * size, positions), BF16),
            pair_weights,
            pair_weights,
            weight,
            weight,
            back_weights,
            back_weights,
            *sum_buffers(4),
            *sum_buffers(2),
            pltpu.SemaphoreType.DMA((24,)),
        ],
        compiler_params=pltpu.CompilerParams(
            collective_id=1, has_side_effects=True, vmem_limit_bytes=50 * 2**20
        ),
        name="triangle",
    )(
        pair,
        cotangent,
        pad_mask,
        crop_mask,
        pad_mask.reshape(cols, wide),
        crop_mask.reshape(cols, wide),
        left_proj,
        left_gate,
        right_proj,
        right_gate,
        out_gate,
        out_proj,
    )


def solution(mesh):
    blocks = P(("rep", "row"), "col", None)
    return jax.shard_map(
        shards,
        mesh=mesh,
        in_specs=(blocks, P("rep"), P("rep"), P(), P(), P(), P(), P(), P(), blocks),
        out_specs=(blocks, blocks, P("rep", None, None)),
        check_vma=False,
    )
```

```python
import functools

import jax
import jax.numpy as jnp
from jax import lax
from jax.experimental import pallas as pl
from jax.experimental.pallas import tpu as pltpu
from jax.sharding import PartitionSpec as P

MESH = pl.DeviceIdType.MESH
F32 = jnp.float32
BF16 = jnp.bfloat16
EPS = 1e-05
PARTS = 2
LEFT, RIGHT, SUMS, GRADS, LEFT_GRADS, RIGHT_GRADS = (PARTS * n for n in range(6))
WEIGHTS_A, WEIGHTS_B = 6 * PARTS, 6 * PARTS + 3


def dot_nn(left, right):
    return jnp.dot(left, right, preferred_element_type=F32)


def dot_nt(left, right):
    return lax.dot_general(left, right, (((1,), (1,)), ((), ())), preferred_element_type=F32)


def dot_tn(left, right):
    return lax.dot_general(left, right, (((0,), (0,)), ((), ())), preferred_element_type=F32)


def mean_rows(values):
    return jnp.mean(values, axis=0, keepdims=True)


def wait_bytes(ref, sem):
    pltpu.make_async_copy(ref, ref, sem).wait()


def kernel(
    rows,
    cols,
    pair_in,
    cot_in,
    pad_in,
    crop_in,
    left_proj_in,
    left_gate_in,
    right_proj_in,
    right_gate_in,
    out_gate_in,
    out_proj_in,
    result,
    grad_pair,
    weight_grads,
    pair,
    cot,
    pad_mask,
    crop_mask,
    left_proj,
    left_gate,
    right_proj,
    right_gate,
    out_gate,
    out_proj,
    in_sems,
    send_l,
    send_r,
    send_s,
    send_g,
    send_dl,
    send_dr,
    recv_l,
    recv_r,
    recv_s,
    recv_g,
    recv_dl,
    recv_dr,
    stage,
    spread,
    mat_l,
    mat_g,
    norm_t,
    xhat,
    scale,
    left_v,
    left_s,
    right_v,
    right_s,
    gate_c,
    gate_u,
    grad_ns,
    grad_n,
    norm_s,
    grad_p,
    grad_o,
    grad_e,
    w_left,
    w_right,
    w_out,
    w_proj,
    b_left,
    b_right,
    part_a,
    held_a,
    line_a,
    full_a,
    part_b,
    held_b,
    line_b,
    full_b,
    sems,
):
    row, col = lax.axis_index("row"), lax.axis_index("col")
    me = row * cols + col
    channels = rows * cols
    tiles, half_lanes = pair.shape[0] // 2, pair.shape[1]
    width, part_tiles, per = 2 * half_lanes, tiles // PARTS, rows // cols
    strip = rows * part_tiles
    order = sorted(range(cols), key=lambda step: min(step, cols - step))
    barrier = pltpu.get_barrier_semaphore()

    fetches = [
        pltpu.make_async_copy(source, target, in_sems.at[n])
        for n, (source, target) in enumerate(
            (
                (pair_in, pair),
                (right_proj_in, right_proj),
                (right_gate_in, right_gate),
                (pad_in, pad_mask),
                (left_proj_in, left_proj),
                (left_gate_in, left_gate),
                (crop_in, crop_mask),
                (out_gate_in, out_gate),
                (out_proj_in, out_proj),
                (cot_in, cot),
            )
        )
    ]
    for fetch in fetches:
        fetch.start()

    def device(r, c):
        return {"row": r, "col": c}

    def for_rows(act, itself):
        def step(shift, carry):
            act(lax.rem(row + shift, rows))
            return carry

        lax.fori_loop(0 if itself else 1, rows, step, 0)

    def for_peers(act):
        def step(shift, carry):
            for hop in order[1:]:
                act(lax.rem(row + shift, rows), lax.rem(col + hop, cols))

            @pl.when(shift > 0)
            def _():
                act(lax.rem(row + shift, rows), col)

            return carry

        lax.fori_loop(0, rows, step, 0)

    for_peers(
        lambda r, c: pl.semaphore_signal(
            barrier, inc=1, device_id=device(r, c), device_id_type=MESH
        )
    )

    def copy_to(src, dst, which, r, c):
        pltpu.make_async_remote_copy(
            src_ref=src,
            dst_ref=dst,
            send_sem=sems.at[2 * which],
            recv_sem=sems.at[2 * which + 1],
            device_id=device(r, c),
            device_id_type=MESH,
        ).start()

    def to_owners(src, dst, which, part):
        dst[part, col, row] = src[part, me]
        for_peers(
            lambda r, c: copy_to(
                src.at[part, r * cols + c], dst.at[part, col, row], which + part, r, c
            )
        )

    def from_owner(src, dst, which, part, r, c):
        copy_to(src.at[part, c, r], dst.at[part, me], which + part, r, c)

    def keep_own(src, dst, part):
        dst[part, me] = src[part, col, row]

    def arrived(which, part):
        wait_bytes(send_l.at[0, pl.ds(0, channels - 1)], sems.at[2 * (which + part) + 1])

    def sent(which):
        wait_bytes(send_l.at[0, pl.ds(0, channels - 1)], sems.at[2 * which])

    def for_tiles(part, body):
        def step(q, carry):
            body(part * part_tiles + q, q)
            return carry

        lax.fori_loop(0, part_tiles, step, 0, unroll=2)

    def lanes(p):
        return pl.ds(pl.multiple_of(p * width, width), width)

    def strided(q):
        return pl.ds(q, channels, stride=part_tiles)

    def part_lanes(part):
        return pl.ds(part * part_tiles * width, part_tiles * width)

    def pack(dst, part):
        dst[part] = stage[...].reshape(channels, part_tiles, width).astype(BF16)

    def unpack(src, part):
        stage[...] = src[part].astype(F32).reshape(channels * part_tiles, width)

    lane = lax.broadcasted_iota(jnp.int32, (1, width), 1)
    low = lane < half_lanes

    def mask_of(ref):
        def put(n, line):
            value = ref[col * half_lanes + n].astype(F32)
            hit = jnp.logical_or(lane == n, lane == n + half_lanes)
            return jnp.where(hit, value, line)

        line = lax.fori_loop(0, half_lanes, put, jnp.zeros((1, width), F32), unroll=4)

        def mask(p):
            first = ref[row * 2 * tiles + p].astype(F32)
            second = ref[row * 2 * tiles + tiles + p].astype(F32)
            return jnp.where(low, first, second) * line

        return mask

    def tile_t(ref, p):
        both = jnp.concatenate([ref[p], ref[p + tiles]], axis=0)
        return both.astype(F32).T

    def put_tile(ref, p, values):
        back = values.T.astype(BF16)
        ref[p] = back[:half_lanes]
        ref[p + tiles] = back[half_lanes:]

    def flip(ref):
        return ref[...].astype(F32).T.astype(BF16)

    size = left_proj.shape[0]
    for fetch in fetches[:4]:
        fetch.wait()
    w_right[:size] = flip(right_proj)
    w_right[size:] = flip(right_gate)
    pad = mask_of(pad_mask)

    def edge(p, q, normed, weight, value_ref, sig_ref):
        both = dot_nn(weight[...], normed)
        value, sig = both[:size], jax.nn.sigmoid(both[size:])
        value_ref[p] = value
        sig_ref[p] = sig
        stage[strided(q), :] = pad(p) * sig * value

    def right_tile(p, q):
        wide = tile_t(pair, p)
        center = wide - mean_rows(wide)
        rstd = lax.rsqrt(mean_rows(center * center) + EPS)
        hat = center * rstd
        xhat[p] = hat
        scale[p] = rstd
        normed = hat.astype(BF16)
        norm_t[:, lanes(p)] = normed
        edge(p, q, normed, w_right, right_v, right_s)

    def left_tile(p, q):
        edge(p, q, norm_t[:, lanes(p)], w_left, left_v, left_s)

    for part in range(PARTS):
        for_tiles(part, right_tile)
        pack(send_r, part)
        if part == 0:
            pl.semaphore_wait(barrier, channels - 1)
        to_owners(send_r, recv_r, RIGHT, part)
    for fetch in fetches[4:]:
        fetch.wait()
    w_left[:size] = flip(left_proj)
    w_left[size:] = flip(left_gate)
    for part in range(PARTS):
        for_tiles(part, left_tile)
        pack(send_l, part)
        to_owners(send_l, recv_l, LEFT, part)

    w_out[...] = flip(out_gate)
    w_proj[...] = flip(out_proj)
    b_left[:, :size] = left_proj[...]
    b_left[:, size:] = left_gate[...]
    b_right[:, :size] = right_proj[...]
    b_right[:, size:] = right_gate[...]
    crop = mask_of(crop_mask)

    def out_tile(p, q):
        gate = jax.nn.sigmoid(dot_nn(w_out[...], norm_t[:, lanes(p)]))
        upstream = crop(p) * tile_t(cot, p)
        projected_grad = (upstream * gate).astype(BF16)
        grad_p[:, lanes(p)] = projected_grad
        gate_c[p] = crop(p) * gate
        gate_u[p] = upstream * gate * (1.0 - gate)
        grad_ns[p] = dot_nn(out_proj[...], projected_grad)

    for part in range(PARTS):
        for_tiles(part, out_tile)

    for part in range(PARTS):
        arrived(RIGHT, part)

    def spread_block(k, carry):
        for c in range(cols):
            raw = recv_r[:, k, c * per : (c + 1) * per].astype(F32)
            turned = pltpu.roll(raw.reshape(PARTS * per * part_tiles, width), half_lanes, 1)
            turned = turned.reshape(raw.shape)
            pieces = []
            for half in range(2):
                for r in range(per):
                    for own in range(2):
                        for part in range(PARTS):
                            piece = raw[part, r] if half == own else turned[part, r]
                            keep = low if half == 0 else jnp.logical_not(low)
                            pieces.append(jnp.where(keep, piece, 0.0))
            block = jnp.concatenate(pieces, axis=0).astype(BF16)
            spread[c * width : (c + 1) * width, lanes(k)] = block
        return carry

    lax.fori_loop(0, cols, spread_block, 0)

    def gather(src, dst, part):
        for c in range(cols):
            block = src[part, c].astype(F32).reshape(strip, width).astype(BF16)
            dst[part * strip : (part + 1) * strip, c * width : (c + 1) * width] = block

    def send_strip(src, dst, which, part, hop, c, values):
        src[part, c] = values.reshape(rows, part_tiles, width).astype(BF16)
        for_rows(lambda r: from_owner(src, dst, which, part, r, c), hop != 0)

    def strip_of(mat, part):
        return mat[part * strip : (part + 1) * strip, :]

    hops = order[1:] + order[:1]
    for part in range(PARTS):
        arrived(LEFT, part)
        gather(recv_l, mat_l, part)
        for hop in hops:
            c = lax.rem(col + hop, cols)
            sums = dot_nt(strip_of(mat_l, part), spread[lanes(c), :])
            send_strip(send_s, recv_s, SUMS, part, hop, c, sums)
        keep_own(send_s, recv_s, part)

    def sum_tile(p, q):
        sums = stage[strided(q), :]
        center = sums - mean_rows(sums)
        rstd = lax.rsqrt(mean_rows(center * center) + EPS)
        hat = center * rstd
        norm_s[:, lanes(p)] = hat.astype(BF16)
        grad = grad_ns[p]
        grad = rstd * (grad - mean_rows(grad) - hat * mean_rows(grad * hat))
        stage[strided(q), :] = grad

    for part in range(PARTS):
        arrived(SUMS, part)
        unpack(recv_s, part)
        for_tiles(part, sum_tile)
        pack(send_g, part)
        to_owners(send_g, recv_g, GRADS, part)

    def result_tile(p, q):
        projected = dot_nn(w_proj[...], norm_s[:, lanes(p)])
        put_tile(result, p, gate_c[p] * projected)
        logit = (gate_u[p] * projected).astype(BF16)
        grad_o[:, lanes(p)] = logit
        grad_n[p] = dot_nn(out_gate[...], logit)

    for part in range(PARTS):
        for_tiles(part, result_tile)
        arrived(GRADS, part)
        gather(recv_g, mat_g, part)
        for hop in hops:
            c = lax.rem(col + hop, cols)
            grads = dot_nn(strip_of(mat_g, part), spread[:, lanes(c)])
            send_strip(send_dl, recv_dl, LEFT_GRADS, part, hop, c, grads)
        keep_own(send_dl, recv_dl, part)

    def right_block(c, carry):
        outer = dot_tn(mat_g[:, lanes(c)], mat_l[...])
        for k in range(cols):
            block = outer[:, k * width : (k + 1) * width]
            block = block.reshape(2, per, 2, tiles, width)
            keep = jnp.where(low, block[0, :, 0], block[1, :, 1])
            turn = jnp.where(low, block[0, :, 1], block[1, :, 0])
            turn = pltpu.roll(turn.reshape(per * tiles, width), half_lanes, 1)
            total = (keep.reshape(per * tiles, width) + turn).reshape(
                per, PARTS, part_tiles, width
            )
            for part in range(PARTS):
                send_dr[part, k, pl.ds(c * per, per)] = total[:, part].astype(BF16)
        return carry

    lax.fori_loop(0, cols, right_block, 0)
    for part in range(PARTS):
        for_peers(lambda r, c: from_owner(send_dr, recv_dr, RIGHT_GRADS, part, r, c))
        keep_own(send_dr, recv_dr, part)

    inverse = 1.0 / (rows * 2 * tiles)

    def put_weight(ref, place, values):
        high = size // rows
        ref[:, place * high : (place + 1) * high, :] = (values * inverse).reshape(
            rows, high, size
        )

    def weight_parts(part, held, which):
        held[row] = part[row]
        for_rows(lambda r: copy_to(part.at[r], held.at[row], which, r, col), False)

    def weight_lines(held, line, which):
        wait_bytes(held.at[pl.ds(0, rows - 1)], sems.at[2 * which + 1])
        line[col] = jnp.sum(held[...], axis=0)
        for hop in order[1:]:
            copy_to(line.at[col], line.at[col], which + 1, row, lax.rem(col + hop, cols))

    def weight_full(line, full, which):
        wait_bytes(line.at[pl.ds(0, cols - 1)], sems.at[2 * which + 3])
        full[row] = jnp.sum(line[...], axis=0)
        for_rows(lambda r: copy_to(full.at[row], full.at[row], which + 2, r, col), False)

    def weight_done(line, full, which, places):
        wait_bytes(full.at[pl.ds(0, rows - 1)], sems.at[2 * which + 5])
        high = size // rows
        for slot, place in enumerate(places):
            part = full[:, slot * high : (slot + 1) * high, :]
            weight_grads[place] = part.reshape(size, size)
        wait_bytes(full.at[pl.ds(0, rows - 1)], sems.at[2 * which])
        wait_bytes(line.at[pl.ds(0, cols - 1)], sems.at[2 * which + 2])
        wait_bytes(full.at[pl.ds(0, rows - 1)], sems.at[2 * which + 4])

    def edge_grads(p, q, value_ref, sig_ref):
        grad, sig = pad(p) * stage[strided(q), :], sig_ref[p]
        grad_v = grad * sig
        grad_e[:size, lanes(p)] = grad_v.astype(BF16)
        grad_e[size:, lanes(p)] = (grad_v * value_ref[p] * (1.0 - sig)).astype(BF16)

    def left_back(p, q):
        edge_grads(p, q, left_v, left_s)
        grad_n[p] += dot_nn(b_left[...], grad_e[:, lanes(p)])

    def right_back(p, q):
        edge_grads(p, q, right_v, right_s)

    def edge_weights(part):
        return dot_nt(norm_t[:, part_lanes(part)], grad_e[:, part_lanes(part)])

    def pair_tile(p, q):
        grad = grad_n[p] + dot_nn(b_right[...], grad_e[:, lanes(p)])
        hat = xhat[p]
        grad = scale[p] * (grad - mean_rows(grad) - hat * mean_rows(grad * hat))
        put_tile(grad_pair, p, grad)

    put_weight(part_a, 2, dot_nt(norm_t[...], grad_o[...]))
    put_weight(part_a, 3, dot_nt(norm_s[...], grad_p[...]))
    total = None
    for part in range(PARTS):
        arrived(LEFT_GRADS, part)
        unpack(recv_dl, part)
        for_tiles(part, left_back)
        both = edge_weights(part)
        total = both if part == 0 else total + both
    put_weight(part_a, 0, total[:, :size])
    put_weight(part_a, 1, total[:, size:])
    weight_parts(part_a, held_a, WEIGHTS_A)
    for part in range(PARTS):
        arrived(RIGHT_GRADS, part)
        unpack(recv_dr, part)
        for_tiles(part, right_back)
        both = edge_weights(part)
        total = both if part == 0 else total + both
        if part < PARTS - 1:
            for_tiles(part, pair_tile)
            weight_lines(held_a, line_a, WEIGHTS_A)
    put_weight(part_b, 0, total[:, :size])
    put_weight(part_b, 1, total[:, size:])
    weight_parts(part_b, held_b, WEIGHTS_B)
    weight_full(line_a, full_a, WEIGHTS_A)
    weight_lines(held_b, line_b, WEIGHTS_B)
    for_tiles(PARTS - 1, pair_tile)
    weight_full(line_b, full_b, WEIGHTS_B)
    weight_done(line_a, full_a, WEIGHTS_A, (0, 1, 4, 5))
    weight_done(line_b, full_b, WEIGHTS_B, (2, 3))
    for which in range(6 * PARTS):
        sent(which)


def shards(
    pair,
    pad_mask,
    crop_mask,
    left_proj,
    left_gate,
    right_proj,
    right_gate,
    out_gate,
    out_proj,
    cotangent,
):
    rows, cols = lax.axis_size("row"), lax.axis_size("col")
    high, wide, size = pair.shape
    tiles, width, channels = high // 2, 2 * wide, rows * cols
    positions = tiles * width
    vmem = pl.BlockSpec(memory_space=pltpu.VMEM)
    hbm = pl.BlockSpec(memory_space=pltpu.HBM)
    at_home = pltpu.VMEM((PARTS, channels, tiles // PARTS, width), BF16)
    at_owner = pltpu.VMEM((PARTS, cols, rows, tiles // PARTS, width), BF16)
    wide_tiles = pltpu.VMEM((tiles, size, width), F32)
    flat = pltpu.VMEM((size, positions), BF16)
    pair_weights = pltpu.VMEM((2 * size, size), BF16)
    weight = pltpu.VMEM((size, size), BF16)
    back_weights = pltpu.VMEM((size, 2 * size), BF16)
    share = size // rows

    def sum_buffers(count):
        return [
            pltpu.VMEM((rows, count * share, size), F32),
            pltpu.VMEM((rows, count * share, size), F32),
            pltpu.VMEM((cols, count * share, size), F32),
            pltpu.VMEM((rows, count * share, size), F32),
        ]

    return pl.pallas_call(
        functools.partial(kernel, rows, cols),
        out_shape=(
            jax.ShapeDtypeStruct(pair.shape, BF16),
            jax.ShapeDtypeStruct(pair.shape, BF16),
            jax.ShapeDtypeStruct((6, size, size), F32),
        ),
        in_specs=[hbm] * 10,
        out_specs=(vmem, vmem, vmem),
        scratch_shapes=[
            pltpu.VMEM(pair.shape, BF16),
            pltpu.VMEM(pair.shape, BF16),
            pltpu.SMEM(pad_mask.shape, jnp.int32),
            pltpu.SMEM(pad_mask.shape, jnp.int32),
            *[weight] * 6,
            pltpu.SemaphoreType.DMA((10,)),
            at_home,
            at_home,
            at_owner,
            at_home,
            at_owner,
            at_owner,
            at_owner,
            at_owner,
            at_home,
            at_owner,
            at_home,
            at_home,
            pltpu.VMEM((channels * tiles // PARTS, width), F32),
            pltpu.VMEM((cols * width, cols * width), BF16),
            pltpu.VMEM((rows * tiles, cols * width), BF16),
            pltpu.VMEM((rows * tiles, cols * width), BF16),
            flat,
            wide_tiles,
            pltpu.VMEM((tiles, 1, width), F32),
            wide_tiles,
            wide_tiles,
            wide_tiles,
            wide_tiles,
            wide_tiles,
            wide_tiles,
            wide_tiles,
            wide_tiles,
            flat,
            flat,
            flat,
            pltpu.VMEM((2 * size, positions), BF16),
            pair_weights,
            pair_weights,
            weight,
            weight,
            back_weights,
            back_weights,
            *sum_buffers(4),
            *sum_buffers(2),
            pltpu.SemaphoreType.DMA((2 * (WEIGHTS_B + 3),)),
        ],
        compiler_params=pltpu.CompilerParams(
            collective_id=1, has_side_effects=True, vmem_limit_bytes=50 * 2**20
        ),
        name="triangle",
    )(
        pair,
        cotangent,
        pad_mask,
        crop_mask,
        left_proj,
        left_gate,
        right_proj,
        right_gate,
        out_gate,
        out_proj,
    )


def solution(mesh):
    blocks = P(("rep", "row"), "col", None)
    return jax.shard_map(
        shards,
        mesh=mesh,
        in_specs=(blocks, P("rep"), P("rep"), P(), P(), P(), P(), P(), P(), blocks),
        out_specs=(blocks, blocks, P("rep", None, None)),
        check_vma=False,
    )
```

```python
import functools

import jax
import jax.numpy as jnp
from jax import lax
from jax.experimental import pallas as pl
from jax.experimental.pallas import tpu as pltpu
from jax.sharding import PartitionSpec as P

MESH = pl.DeviceIdType.MESH
F32 = jnp.float32
BF16 = jnp.bfloat16
EPS = 1e-05
PARTS = 2
VMEM_BYTES = 60 * 2**20
LEFT, RIGHT, SUMS, GRADS, LEFT_GRADS, RIGHT_GRADS = (PARTS * n for n in range(6))
WEIGHTS_A, WEIGHTS_B = 6 * PARTS, 6 * PARTS + 3


def dot_nn(left, right):
    return jnp.dot(left, right, preferred_element_type=F32)


def dot_nt(left, right):
    return lax.dot_general(left, right, (((1,), (1,)), ((), ())), preferred_element_type=F32)


def dot_tn(left, right):
    return lax.dot_general(left, right, (((0,), (0,)), ((), ())), preferred_element_type=F32)


def mean_rows(values):
    return jnp.mean(values, axis=0, keepdims=True)


def wait_bytes(ref, sem):
    pltpu.make_async_copy(ref, ref, sem).wait()


def kernel(
    rows,
    cols,
    pair_in,
    cot_in,
    pad_in,
    crop_in,
    left_proj_in,
    left_gate_in,
    right_proj_in,
    right_gate_in,
    out_gate_in,
    out_proj_in,
    result_out,
    grad_pair_out,
    weight_grads_out,
    result,
    grad_pair,
    weight_grads,
    pair,
    cot,
    pad_mask,
    crop_mask,
    left_proj,
    left_gate,
    right_proj,
    right_gate,
    out_gate,
    out_proj,
    in_sems,
    out_sems,
    send_l,
    send_r,
    send_s,
    send_g,
    send_dl,
    send_dr,
    recv_l,
    recv_r,
    recv_s,
    recv_g,
    recv_dl,
    recv_dr,
    stage,
    spread,
    mat_l,
    mat_g,
    norm_t,
    xhat,
    scale,
    left_v,
    left_s,
    right_v,
    right_s,
    gate_c,
    gate_u,
    grad_ns,
    grad_n,
    norm_s,
    grad_p,
    grad_o,
    grad_e,
    w_left,
    w_right,
    w_out,
    w_proj,
    b_left,
    b_right,
    part_a,
    held_a,
    line_a,
    full_a,
    part_b,
    held_b,
    line_b,
    full_b,
    sems,
):
    row, col = lax.axis_index("row"), lax.axis_index("col")
    me = row * cols + col
    channels = rows * cols
    tiles, half_lanes = pair.shape[0] // 2, pair.shape[1]
    width, part_tiles, per = 2 * half_lanes, tiles // PARTS, rows // cols
    strip = rows * part_tiles
    order = sorted(range(cols), key=lambda step: min(step, cols - step))
    barrier = pltpu.get_barrier_semaphore()

    fetches = [
        pltpu.make_async_copy(source, target, in_sems.at[n])
        for n, (source, target) in enumerate(
            (
                (pair_in, pair),
                (right_proj_in, right_proj),
                (right_gate_in, right_gate),
                (pad_in, pad_mask),
                (left_proj_in, left_proj),
                (left_gate_in, left_gate),
                (crop_in, crop_mask),
                (out_gate_in, out_gate),
                (out_proj_in, out_proj),
                (cot_in, cot),
            )
        )
    ]
    for fetch in fetches:
        fetch.start()
    stores = [
        pltpu.make_async_copy(source, target, out_sems.at[n])
        for n, (source, target) in enumerate(
            (
                (result, result_out),
                (grad_pair, grad_pair_out),
                (weight_grads, weight_grads_out),
            )
        )
    ]

    def device(r, c):
        return {"row": r, "col": c}

    def for_rows(act, itself):
        def step(shift, carry):
            act(lax.rem(row + shift, rows))
            return carry

        lax.fori_loop(0 if itself else 1, rows, step, 0)

    def for_peers(act):
        def step(shift, carry):
            for hop in order[1:]:
                act(lax.rem(row + shift, rows), lax.rem(col + hop, cols))

            @pl.when(shift > 0)
            def _():
                act(lax.rem(row + shift, rows), col)

            return carry

        lax.fori_loop(0, rows, step, 0)

    for_peers(
        lambda r, c: pl.semaphore_signal(
            barrier, inc=1, device_id=device(r, c), device_id_type=MESH
        )
    )

    def copy_to(src, dst, which, r, c):
        pltpu.make_async_remote_copy(
            src_ref=src,
            dst_ref=dst,
            send_sem=sems.at[2 * which],
            recv_sem=sems.at[2 * which + 1],
            device_id=device(r, c),
            device_id_type=MESH,
        ).start()

    def to_owners(src, dst, which, part):
        dst[part, col, row] = src[part, me]
        for_peers(
            lambda r, c: copy_to(
                src.at[part, r * cols + c], dst.at[part, col, row], which + part, r, c
            )
        )

    def from_owner(src, dst, which, part, r, c):
        copy_to(src.at[part, c, r], dst.at[part, me], which + part, r, c)

    def keep_own(src, dst, part):
        dst[part, me] = src[part, col, row]

    def arrived(which, part):
        wait_bytes(send_l.at[0, pl.ds(0, channels - 1)], sems.at[2 * (which + part) + 1])

    def sent(which):
        wait_bytes(send_l.at[0, pl.ds(0, channels - 1)], sems.at[2 * which])

    def for_tiles(part, body):
        def step(q, carry):
            body(part * part_tiles + q, q)
            return carry

        lax.fori_loop(0, part_tiles, step, 0, unroll=2)

    def lanes(p):
        return pl.ds(pl.multiple_of(p * width, width), width)

    def strided(q):
        return pl.ds(q, channels, stride=part_tiles)

    def part_lanes(part):
        return pl.ds(part * part_tiles * width, part_tiles * width)

    def pack(dst, part):
        dst[part] = stage[...].reshape(channels, part_tiles, width).astype(BF16)

    def unpack(src, part):
        stage[...] = src[part].astype(F32).reshape(channels * part_tiles, width)

    lane = lax.broadcasted_iota(jnp.int32, (1, width), 1)
    low = lane < half_lanes

    def mask_of(ref):
        def put(n, line):
            value = ref[col * half_lanes + n].astype(F32)
            hit = jnp.logical_or(lane == n, lane == n + half_lanes)
            return jnp.where(hit, value, line)

        line = lax.fori_loop(0, half_lanes, put, jnp.zeros((1, width), F32), unroll=4)

        def mask(p):
            first = ref[row * 2 * tiles + p].astype(F32)
            second = ref[row * 2 * tiles + tiles + p].astype(F32)
            return jnp.where(low, first, second) * line

        return mask

    def tile_t(ref, p):
        both = jnp.concatenate([ref[p], ref[p + tiles]], axis=0)
        return both.astype(F32).T

    def put_tile(ref, p, values):
        back = values.T.astype(BF16)
        ref[p] = back[:half_lanes]
        ref[p + tiles] = back[half_lanes:]

    def flip(ref):
        return ref[...].astype(F32).T.astype(BF16)

    size = left_proj.shape[0]
    for fetch in fetches[:4]:
        fetch.wait()
    w_right[:size] = flip(right_proj)
    w_right[size:] = flip(right_gate)
    pad = mask_of(pad_mask)

    def edge(p, q, normed, weight, value_ref, sig_ref):
        both = dot_nn(weight[...], normed)
        value, sig = both[:size], jax.nn.sigmoid(both[size:])
        value_ref[p] = value
        sig_ref[p] = sig
        stage[strided(q), :] = pad(p) * sig * value

    def right_tile(p, q):
        wide = tile_t(pair, p)
        center = wide - mean_rows(wide)
        rstd = lax.rsqrt(mean_rows(center * center) + EPS)
        hat = center * rstd
        xhat[p] = hat
        scale[p] = rstd
        normed = hat.astype(BF16)
        norm_t[:, lanes(p)] = normed
        edge(p, q, normed, w_right, right_v, right_s)

    def left_tile(p, q):
        edge(p, q, norm_t[:, lanes(p)], w_left, left_v, left_s)

    for part in range(PARTS):
        for_tiles(part, right_tile)
        pack(send_r, part)
        if part == 0:
            pl.semaphore_wait(barrier, channels - 1)
        to_owners(send_r, recv_r, RIGHT, part)
    for fetch in fetches[4:]:
        fetch.wait()
    w_left[:size] = flip(left_proj)
    w_left[size:] = flip(left_gate)
    for part in range(PARTS):
        for_tiles(part, left_tile)
        pack(send_l, part)
        to_owners(send_l, recv_l, LEFT, part)

    w_out[...] = flip(out_gate)
    w_proj[...] = flip(out_proj)
    b_left[:, :size] = left_proj[...]
    b_left[:, size:] = left_gate[...]
    b_right[:, :size] = right_proj[...]
    b_right[:, size:] = right_gate[...]
    crop = mask_of(crop_mask)

    def out_tile(p, q):
        gate = jax.nn.sigmoid(dot_nn(w_out[...], norm_t[:, lanes(p)]))
        upstream = crop(p) * tile_t(cot, p)
        projected_grad = (upstream * gate).astype(BF16)
        grad_p[:, lanes(p)] = projected_grad
        gate_c[p] = crop(p) * gate
        gate_u[p] = upstream * gate * (1.0 - gate)
        grad_ns[p] = dot_nn(out_proj[...], projected_grad)

    for part in range(PARTS):
        for_tiles(part, out_tile)

    for part in range(PARTS):
        arrived(RIGHT, part)

    def spread_block(k, carry):
        for c in range(cols):
            raw = recv_r[:, k, c * per : (c + 1) * per].astype(F32)
            turned = pltpu.roll(raw.reshape(PARTS * per * part_tiles, width), half_lanes, 1)
            turned = turned.reshape(raw.shape)
            pieces = []
            for half in range(2):
                for r in range(per):
                    for own in range(2):
                        for part in range(PARTS):
                            piece = raw[part, r] if half == own else turned[part, r]
                            keep = low if half == 0 else jnp.logical_not(low)
                            pieces.append(jnp.where(keep, piece, 0.0))
            block = jnp.concatenate(pieces, axis=0).astype(BF16)
            spread[c * width : (c + 1) * width, lanes(k)] = block
        return carry

    lax.fori_loop(0, cols, spread_block, 0)

    def gather(src, dst, part):
        for c in range(cols):
            block = src[part, c].astype(F32).reshape(strip, width).astype(BF16)
            dst[part * strip : (part + 1) * strip, c * width : (c + 1) * width] = block

    def send_strip(src, dst, which, part, hop, c, values):
        src[part, c] = values.reshape(rows, part_tiles, width).astype(BF16)
        for_rows(lambda r: from_owner(src, dst, which, part, r, c), hop != 0)

    def strip_of(mat, part):
        return mat[part * strip : (part + 1) * strip, :]

    hops = order[1:] + order[:1]
    for part in range(PARTS):
        arrived(LEFT, part)
        gather(recv_l, mat_l, part)
        for hop in hops:
            c = lax.rem(col + hop, cols)
            sums = dot_nt(strip_of(mat_l, part), spread[lanes(c), :])
            send_strip(send_s, recv_s, SUMS, part, hop, c, sums)
        keep_own(send_s, recv_s, part)

    def sum_tile(p, q):
        sums = stage[strided(q), :]
        center = sums - mean_rows(sums)
        rstd = lax.rsqrt(mean_rows(center * center) + EPS)
        hat = center * rstd
        norm_s[:, lanes(p)] = hat.astype(BF16)
        grad = grad_ns[p]
        grad = rstd * (grad - mean_rows(grad) - hat * mean_rows(grad * hat))
        stage[strided(q), :] = grad

    for part in range(PARTS):
        arrived(SUMS, part)
        unpack(recv_s, part)
        for_tiles(part, sum_tile)
        pack(send_g, part)
        to_owners(send_g, recv_g, GRADS, part)

    def result_tile(p, q):
        projected = dot_nn(w_proj[...], norm_s[:, lanes(p)])
        put_tile(result, p, gate_c[p] * projected)
        logit = (gate_u[p] * projected).astype(BF16)
        grad_o[:, lanes(p)] = logit
        grad_n[p] = dot_nn(out_gate[...], logit)

    for part in range(PARTS):
        for_tiles(part, result_tile)
        arrived(GRADS, part)
        gather(recv_g, mat_g, part)
        for hop in hops:
            c = lax.rem(col + hop, cols)
            grads = dot_nn(strip_of(mat_g, part), spread[:, lanes(c)])
            send_strip(send_dl, recv_dl, LEFT_GRADS, part, hop, c, grads)
        keep_own(send_dl, recv_dl, part)

    def right_block(c, carry):
        outer = dot_tn(mat_g[:, lanes(c)], mat_l[...])
        for k in range(cols):
            block = outer[:, k * width : (k + 1) * width]
            block = block.reshape(2, per, 2, tiles, width)
            keep = jnp.where(low, block[0, :, 0], block[1, :, 1])
            turn = jnp.where(low, block[0, :, 1], block[1, :, 0])
            turn = pltpu.roll(turn.reshape(per * tiles, width), half_lanes, 1)
            total = (keep.reshape(per * tiles, width) + turn).reshape(
                per, PARTS, part_tiles, width
            )
            for part in range(PARTS):
                send_dr[part, k, pl.ds(c * per, per)] = total[:, part].astype(BF16)
        return carry

    lax.fori_loop(0, cols, right_block, 0)
    for part in range(PARTS):
        for_peers(lambda r, c: from_owner(send_dr, recv_dr, RIGHT_GRADS, part, r, c))
        keep_own(send_dr, recv_dr, part)

    stores[0].start()

    inverse = 1.0 / (rows * 2 * tiles)

    def put_weight(ref, place, values):
        high = size // rows
        ref[:, place * high : (place + 1) * high, :] = (values * inverse).reshape(
            rows, high, size
        )

    def weight_parts(part, held, which):
        held[row] = part[row]
        for_rows(lambda r: copy_to(part.at[r], held.at[row], which, r, col), False)

    def weight_lines(held, line, which):
        wait_bytes(held.at[pl.ds(0, rows - 1)], sems.at[2 * which + 1])
        line[col] = jnp.sum(held[...], axis=0)
        for hop in order[1:]:
            copy_to(line.at[col], line.at[col], which + 1, row, lax.rem(col + hop, cols))

    def weight_full(line, full, which):
        wait_bytes(line.at[pl.ds(0, cols - 1)], sems.at[2 * which + 3])
        full[row] = jnp.sum(line[...], axis=0)
        for_rows(lambda r: copy_to(full.at[row], full.at[row], which + 2, r, col), False)

    def weight_done(line, full, which, places):
        wait_bytes(full.at[pl.ds(0, rows - 1)], sems.at[2 * which + 5])
        high = size // rows
        for slot, place in enumerate(places):
            part = full[:, slot * high : (slot + 1) * high, :]
            weight_grads[place] = part.reshape(size, size)
        wait_bytes(full.at[pl.ds(0, rows - 1)], sems.at[2 * which])
        wait_bytes(line.at[pl.ds(0, cols - 1)], sems.at[2 * which + 2])
        wait_bytes(full.at[pl.ds(0, rows - 1)], sems.at[2 * which + 4])

    def edge_grads(p, q, value_ref, sig_ref):
        grad, sig = pad(p) * stage[strided(q), :], sig_ref[p]
        grad_v = grad * sig
        grad_e[:size, lanes(p)] = grad_v.astype(BF16)
        grad_e[size:, lanes(p)] = (grad_v * value_ref[p] * (1.0 - sig)).astype(BF16)

    def left_back(p, q):
        edge_grads(p, q, left_v, left_s)
        grad_n[p] += dot_nn(b_left[...], grad_e[:, lanes(p)])

    def right_back(p, q):
        edge_grads(p, q, right_v, right_s)

    def edge_weights(part):
        return dot_nt(norm_t[:, part_lanes(part)], grad_e[:, part_lanes(part)])

    def pair_tile(p, q):
        grad = grad_n[p] + dot_nn(b_right[...], grad_e[:, lanes(p)])
        hat = xhat[p]
        grad = scale[p] * (grad - mean_rows(grad) - hat * mean_rows(grad * hat))
        put_tile(grad_pair, p, grad)

    put_weight(part_a, 2, dot_nt(norm_t[...], grad_o[...]))
    put_weight(part_a, 3, dot_nt(norm_s[...], grad_p[...]))
    total = None
    for part in range(PARTS):
        arrived(LEFT_GRADS, part)
        unpack(recv_dl, part)
        for_tiles(part, left_back)
        both = edge_weights(part)
        total = both if part == 0 else total + both
    put_weight(part_a, 0, total[:, :size])
    put_weight(part_a, 1, total[:, size:])
    weight_parts(part_a, held_a, WEIGHTS_A)
    for part in range(PARTS):
        arrived(RIGHT_GRADS, part)
        unpack(recv_dr, part)
        for_tiles(part, right_back)
        both = edge_weights(part)
        total = both if part == 0 else total + both
        if part < PARTS - 1:
            for_tiles(part, pair_tile)
            weight_lines(held_a, line_a, WEIGHTS_A)
    put_weight(part_b, 0, total[:, :size])
    put_weight(part_b, 1, total[:, size:])
    weight_parts(part_b, held_b, WEIGHTS_B)
    weight_full(line_a, full_a, WEIGHTS_A)
    weight_lines(held_b, line_b, WEIGHTS_B)
    for_tiles(PARTS - 1, pair_tile)
    stores[1].start()
    weight_full(line_b, full_b, WEIGHTS_B)
    weight_done(line_a, full_a, WEIGHTS_A, (0, 1, 4, 5))
    weight_done(line_b, full_b, WEIGHTS_B, (2, 3))
    stores[2].start()
    for which in range(6 * PARTS):
        sent(which)
    for store in stores:
        store.wait()


def settle_kernel(count, *refs):
    arrays, outs, held, sems = refs[:count], refs[count : 2 * count], refs[2 * count : -1], refs[-1]
    loads = [
        pltpu.make_async_copy(arrays[n], held[n], sems.at[n]) for n in range(count)
    ]
    stores = [
        pltpu.make_async_copy(held[n], outs[n], sems.at[count + n]) for n in range(count)
    ]
    for load in loads:
        load.start()
    for load, store in zip(loads, stores):
        load.wait()
        store.start()
    for store in stores:
        store.wait()


def settle(arrays):
    count = len(arrays)
    hbm = pl.BlockSpec(memory_space=pltpu.HBM)
    return pl.pallas_call(
        functools.partial(settle_kernel, count),
        out_shape=tuple(jax.ShapeDtypeStruct(a.shape, a.dtype) for a in arrays),
        in_specs=[hbm] * count,
        out_specs=(hbm,) * count,
        scratch_shapes=[
            *[pltpu.VMEM(a.shape, a.dtype) for a in arrays],
            pltpu.SemaphoreType.DMA((2 * count,)),
        ],
        compiler_params=pltpu.CompilerParams(vmem_limit_bytes=VMEM_BYTES),
        name="settle",
    )(*arrays)


def shards(
    pair,
    pad_mask,
    crop_mask,
    left_proj,
    left_gate,
    right_proj,
    right_gate,
    out_gate,
    out_proj,
    cotangent,
):
    rows, cols = lax.axis_size("row"), lax.axis_size("col")
    high, wide, size = pair.shape
    tiles, width, channels = high // 2, 2 * wide, rows * cols
    positions = tiles * width
    hbm = pl.BlockSpec(memory_space=pltpu.HBM)
    at_home = pltpu.VMEM((PARTS, channels, tiles // PARTS, width), BF16)
    at_owner = pltpu.VMEM((PARTS, cols, rows, tiles // PARTS, width), BF16)
    wide_tiles = pltpu.VMEM((tiles, size, width), F32)
    flat = pltpu.VMEM((size, positions), BF16)
    pair_weights = pltpu.VMEM((2 * size, size), BF16)
    weight = pltpu.VMEM((size, size), BF16)
    back_weights = pltpu.VMEM((size, 2 * size), BF16)
    share = size // rows

    def sum_buffers(count):
        return [
            pltpu.VMEM((rows, count * share, size), F32),
            pltpu.VMEM((rows, count * share, size), F32),
            pltpu.VMEM((cols, count * share, size), F32),
            pltpu.VMEM((rows, count * share, size), F32),
        ]

    outs = pl.pallas_call(
        functools.partial(kernel, rows, cols),
        out_shape=(
            jax.ShapeDtypeStruct(pair.shape, BF16),
            jax.ShapeDtypeStruct(pair.shape, BF16),
            jax.ShapeDtypeStruct((6, size, size), F32),
        ),
        in_specs=[hbm] * 10,
        out_specs=(hbm, hbm, hbm),
        scratch_shapes=[
            pltpu.VMEM(pair.shape, BF16),
            pltpu.VMEM(pair.shape, BF16),
            pltpu.VMEM((6, size, size), F32),
            pltpu.VMEM(pair.shape, BF16),
            pltpu.VMEM(pair.shape, BF16),
            pltpu.SMEM(pad_mask.shape, jnp.int32),
            pltpu.SMEM(pad_mask.shape, jnp.int32),
            *[weight] * 6,
            pltpu.SemaphoreType.DMA((10,)),
            pltpu.SemaphoreType.DMA((3,)),
            at_home,
            at_home,
            at_owner,
            at_home,
            at_owner,
            at_owner,
            at_owner,
            at_owner,
            at_home,
            at_owner,
            at_home,
            at_home,
            pltpu.VMEM((channels * tiles // PARTS, width), F32),
            pltpu.VMEM((cols * width, cols * width), BF16),
            pltpu.VMEM((rows * tiles, cols * width), BF16),
            pltpu.VMEM((rows * tiles, cols * width), BF16),
            flat,
            wide_tiles,
            pltpu.VMEM((tiles, 1, width), F32),
            wide_tiles,
            wide_tiles,
            wide_tiles,
            wide_tiles,
            wide_tiles,
            wide_tiles,
            wide_tiles,
            wide_tiles,
            flat,
            flat,
            flat,
            pltpu.VMEM((2 * size, positions), BF16),
            pair_weights,
            pair_weights,
            weight,
            weight,
            back_weights,
            back_weights,
            *sum_buffers(4),
            *sum_buffers(2),
            pltpu.SemaphoreType.DMA((2 * (WEIGHTS_B + 3),)),
        ],
        compiler_params=pltpu.CompilerParams(
            collective_id=1, has_side_effects=True, vmem_limit_bytes=VMEM_BYTES
        ),
        name="triangle",
    )(
        pair,
        cotangent,
        pad_mask,
        crop_mask,
        left_proj,
        left_gate,
        right_proj,
        right_gate,
        out_gate,
        out_proj,
    )
    return settle(outs)


def solution(mesh):
    blocks = P(("rep", "row"), "col", None)
    return jax.shard_map(
        shards,
        mesh=mesh,
        in_specs=(blocks, P("rep"), P("rep"), P(), P(), P(), P(), P(), P(), blocks),
        out_specs=(blocks, blocks, P("rep", None, None)),
        check_vma=False,
    )
```

```python
import functools

import jax
import jax.numpy as jnp
from jax import lax
from jax.experimental import pallas as pl
from jax.experimental.pallas import tpu as pltpu
from jax.sharding import PartitionSpec as P

MESH = pl.DeviceIdType.MESH
F32 = jnp.float32
BF16 = jnp.bfloat16
EPS = 1e-05
PARTS = 2
VMEM_BYTES = 50 * 2**20
SETTLE_BYTES = 4 * 2**20
LEFT, RIGHT, SUMS, GRADS, LEFT_GRADS, RIGHT_GRADS = (PARTS * n for n in range(6))
WEIGHTS_O, WEIGHTS_L, WEIGHTS_R = (6 * PARTS + 3 * n for n in range(3))


def dot_nn(left, right):
    return jnp.dot(left, right, preferred_element_type=F32)


def dot_nt(left, right):
    return lax.dot_general(left, right, (((1,), (1,)), ((), ())), preferred_element_type=F32)


def dot_tn(left, right):
    return lax.dot_general(left, right, (((0,), (0,)), ((), ())), preferred_element_type=F32)


def mean_rows(values):
    return jnp.mean(values, axis=0, keepdims=True)


def wait_bytes(ref, sem):
    pltpu.make_async_copy(ref, ref, sem).wait()


def kernel(
    rows,
    cols,
    pair_in,
    cot_in,
    pad_in,
    crop_in,
    left_proj_in,
    left_gate_in,
    right_proj_in,
    right_gate_in,
    out_gate_in,
    out_proj_in,
    result,
    grad_pair,
    weight_grads,
    pair,
    cot,
    pad_mask,
    crop_mask,
    left_proj,
    left_gate,
    right_proj,
    right_gate,
    out_gate,
    out_proj,
    in_sems,
    send_l,
    send_r,
    send_s,
    send_g,
    send_dl,
    send_dr,
    recv_l,
    recv_r,
    recv_s,
    recv_g,
    recv_dl,
    recv_dr,
    stage,
    spread,
    mat_l,
    mat_g,
    norm_t,
    xhat,
    scale,
    left_v,
    left_s,
    right_v,
    right_s,
    gate_c,
    gate_u,
    grad_ns,
    grad_n,
    norm_s,
    grad_p,
    grad_o,
    grad_e,
    w_left,
    w_right,
    w_out,
    w_proj,
    b_left,
    b_right,
    part_o,
    held_o,
    line_o,
    full_o,
    part_l,
    held_l,
    line_l,
    full_l,
    part_r,
    held_r,
    line_r,
    full_r,
    sems,
):
    row, col = lax.axis_index("row"), lax.axis_index("col")
    me = row * cols + col
    channels = rows * cols
    tiles, half_lanes = pair.shape[0] // 2, pair.shape[1]
    width, part_tiles, per = 2 * half_lanes, tiles // PARTS, rows // cols
    strip = rows * part_tiles
    order = sorted(range(cols), key=lambda step: min(step, cols - step))
    barrier = pltpu.get_barrier_semaphore()

    fetches = [
        pltpu.make_async_copy(source, target, in_sems.at[n])
        for n, (source, target) in enumerate(
            (
                (right_proj_in, right_proj),
                (right_gate_in, right_gate),
                (pad_in, pad_mask),
                (pair_in, pair),
                (left_proj_in, left_proj),
                (left_gate_in, left_gate),
                (crop_in, crop_mask),
                (out_gate_in, out_gate),
                (out_proj_in, out_proj),
                (cot_in, cot),
            )
        )
    ]
    for fetch in fetches:
        fetch.start()

    def device(r, c):
        return {"row": r, "col": c}

    def for_rows(act, itself):
        def step(shift, carry):
            act(lax.rem(row + shift, rows))
            return carry

        lax.fori_loop(0 if itself else 1, rows, step, 0)

    def for_peers(act):
        def step(shift, carry):
            for hop in order[1:]:
                act(lax.rem(row + shift, rows), lax.rem(col + hop, cols))

            @pl.when(shift > 0)
            def _():
                act(lax.rem(row + shift, rows), col)

            return carry

        lax.fori_loop(0, rows, step, 0)

    for_peers(
        lambda r, c: pl.semaphore_signal(
            barrier, inc=1, device_id=device(r, c), device_id_type=MESH
        )
    )

    def copy_to(src, dst, which, r, c):
        pltpu.make_async_remote_copy(
            src_ref=src,
            dst_ref=dst,
            send_sem=sems.at[2 * which],
            recv_sem=sems.at[2 * which + 1],
            device_id=device(r, c),
            device_id_type=MESH,
        ).start()

    def to_owners(src, dst, which, part):
        dst[part, col, row] = src[part, me]
        for_peers(
            lambda r, c: copy_to(
                src.at[part, r * cols + c], dst.at[part, col, row], which + part, r, c
            )
        )

    def from_owner(src, dst, which, part, r, c):
        copy_to(src.at[part, c, r], dst.at[part, me], which + part, r, c)

    def keep_own(src, dst, part):
        dst[part, me] = src[part, col, row]

    def arrived(which, part):
        wait_bytes(send_l.at[0, pl.ds(0, channels - 1)], sems.at[2 * (which + part) + 1])

    def sent(which):
        wait_bytes(send_l.at[0, pl.ds(0, channels - 1)], sems.at[2 * which])

    def for_tiles(part, body):
        def step(q, carry):
            body(part * part_tiles + q, q)
            return carry

        lax.fori_loop(0, part_tiles, step, 0, unroll=2)

    def lanes(p):
        return pl.ds(pl.multiple_of(p * width, width), width)

    def strided(q):
        return pl.ds(q, channels, stride=part_tiles)

    def part_lanes(part):
        return pl.ds(part * part_tiles * width, part_tiles * width)

    def pack(dst, part):
        dst[part] = stage[...].reshape(channels, part_tiles, width).astype(BF16)

    def unpack(src, part):
        stage[...] = src[part].astype(F32).reshape(channels * part_tiles, width)

    lane = lax.broadcasted_iota(jnp.int32, (1, width), 1)
    low = lane < half_lanes

    def mask_of(ref):
        def put(n, line):
            value = ref[col * half_lanes + n].astype(F32)
            hit = jnp.logical_or(lane == n, lane == n + half_lanes)
            return jnp.where(hit, value, line)

        line = lax.fori_loop(0, half_lanes, put, jnp.zeros((1, width), F32), unroll=4)

        def mask(p):
            first = ref[row * 2 * tiles + p].astype(F32)
            second = ref[row * 2 * tiles + tiles + p].astype(F32)
            return jnp.where(low, first, second) * line

        return mask

    def tile_t(ref, p):
        both = jnp.concatenate([ref[p], ref[p + tiles]], axis=0)
        return both.astype(F32).T

    def put_tile(ref, p, values):
        back = values.T.astype(BF16)
        ref[p] = back[:half_lanes]
        ref[p + tiles] = back[half_lanes:]

    def flip(ref):
        return ref[...].astype(F32).T.astype(BF16)

    size = left_proj.shape[0]
    for fetch in fetches[:3]:
        fetch.wait()
    w_right[:size] = flip(right_proj)
    w_right[size:] = flip(right_gate)
    pad = mask_of(pad_mask)
    fetches[3].wait()

    def edge(p, q, normed, weight, value_ref, sig_ref):
        both = dot_nn(weight[...], normed)
        value, sig = both[:size], jax.nn.sigmoid(both[size:])
        value_ref[p] = value
        sig_ref[p] = sig
        stage[strided(q), :] = pad(p) * sig * value

    def right_tile(p, q):
        wide = tile_t(pair, p)
        center = wide - mean_rows(wide)
        rstd = lax.rsqrt(mean_rows(center * center) + EPS)
        hat = center * rstd
        xhat[p] = hat
        scale[p] = rstd
        normed = hat.astype(BF16)
        norm_t[:, lanes(p)] = normed
        edge(p, q, normed, w_right, right_v, right_s)

    def left_tile(p, q):
        edge(p, q, norm_t[:, lanes(p)], w_left, left_v, left_s)

    for part in range(PARTS):
        for_tiles(part, right_tile)
        pack(send_r, part)
        if part == 0:
            pl.semaphore_wait(barrier, channels - 1)
        to_owners(send_r, recv_r, RIGHT, part)
    for fetch in fetches[4:]:
        fetch.wait()
    w_left[:size] = flip(left_proj)
    w_left[size:] = flip(left_gate)
    for part in range(PARTS):
        for_tiles(part, left_tile)
        pack(send_l, part)
        to_owners(send_l, recv_l, LEFT, part)

    w_out[...] = flip(out_gate)
    w_proj[...] = flip(out_proj)
    b_left[:, :size] = left_proj[...]
    b_left[:, size:] = left_gate[...]
    b_right[:, :size] = right_proj[...]
    b_right[:, size:] = right_gate[...]
    crop = mask_of(crop_mask)

    def out_tile(p, q):
        gate = jax.nn.sigmoid(dot_nn(w_out[...], norm_t[:, lanes(p)]))
        upstream = crop(p) * tile_t(cot, p)
        projected_grad = (upstream * gate).astype(BF16)
        grad_p[:, lanes(p)] = projected_grad
        gate_c[p] = crop(p) * gate
        gate_u[p] = upstream * gate * (1.0 - gate)
        grad_ns[p] = dot_nn(out_proj[...], projected_grad)

    for part in range(PARTS):
        for_tiles(part, out_tile)

    for part in range(PARTS):
        arrived(RIGHT, part)

    def spread_block(k, carry):
        for c in range(cols):
            raw = recv_r[:, k, c * per : (c + 1) * per].astype(F32)
            turned = pltpu.roll(raw.reshape(PARTS * per * part_tiles, width), half_lanes, 1)
            turned = turned.reshape(raw.shape)
            pieces = []
            for half in range(2):
                for r in range(per):
                    for own in range(2):
                        for part in range(PARTS):
                            piece = raw[part, r] if half == own else turned[part, r]
                            keep = low if half == 0 else jnp.logical_not(low)
                            pieces.append(jnp.where(keep, piece, 0.0))
            block = jnp.concatenate(pieces, axis=0).astype(BF16)
            spread[c * width : (c + 1) * width, lanes(k)] = block
        return carry

    lax.fori_loop(0, cols, spread_block, 0)

    def gather(src, dst, part):
        for c in range(cols):
            block = src[part, c].astype(F32).reshape(strip, width).astype(BF16)
            dst[part * strip : (part + 1) * strip, c * width : (c + 1) * width] = block

    def send_strip(src, dst, which, part, hop, c, values):
        src[part, c] = values.reshape(rows, part_tiles, width).astype(BF16)
        for_rows(lambda r: from_owner(src, dst, which, part, r, c), hop != 0)

    def strip_of(mat, part):
        return mat[part * strip : (part + 1) * strip, :]

    hops = order[::-1]
    for part in range(PARTS):
        arrived(LEFT, part)
        gather(recv_l, mat_l, part)
        for hop in hops:
            c = lax.rem(col + hop, cols)
            sums = dot_nt(strip_of(mat_l, part), spread[lanes(c), :])
            send_strip(send_s, recv_s, SUMS, part, hop, c, sums)
        keep_own(send_s, recv_s, part)

    def sum_tile(p, q):
        sums = stage[strided(q), :]
        center = sums - mean_rows(sums)
        rstd = lax.rsqrt(mean_rows(center * center) + EPS)
        hat = center * rstd
        norm_s[:, lanes(p)] = hat.astype(BF16)
        grad = grad_ns[p]
        grad = rstd * (grad - mean_rows(grad) - hat * mean_rows(grad * hat))
        stage[strided(q), :] = grad

    for part in range(PARTS):
        arrived(SUMS, part)
        unpack(recv_s, part)
        for_tiles(part, sum_tile)
        pack(send_g, part)
        to_owners(send_g, recv_g, GRADS, part)

    def result_tile(p, q):
        projected = dot_nn(w_proj[...], norm_s[:, lanes(p)])
        put_tile(result, p, gate_c[p] * projected)
        logit = (gate_u[p] * projected).astype(BF16)
        grad_o[:, lanes(p)] = logit
        grad_n[p] = dot_nn(out_gate[...], logit)

    inverse = 1.0 / (rows * 2 * tiles)

    def put_weight(ref, place, values):
        high = size // rows
        ref[:, place * high : (place + 1) * high, :] = (values * inverse).reshape(
            rows, high, size
        )

    def weight_parts(part, held, which):
        held[row] = part[row]
        for_rows(lambda r: copy_to(part.at[r], held.at[row], which, r, col), False)

    def weight_lines(held, line, which):
        wait_bytes(held.at[pl.ds(0, rows - 1)], sems.at[2 * which + 1])
        line[col] = jnp.sum(held[...], axis=0)
        for hop in order[1:]:
            copy_to(line.at[col], line.at[col], which + 1, row, lax.rem(col + hop, cols))

    def weight_full(line, full, which):
        wait_bytes(line.at[pl.ds(0, cols - 1)], sems.at[2 * which + 3])
        full[row] = jnp.sum(line[...], axis=0)
        for_rows(lambda r: copy_to(full.at[row], full.at[row], which + 2, r, col), False)

    def weight_store(full, which, places):
        wait_bytes(full.at[pl.ds(0, rows - 1)], sems.at[2 * which + 5])
        high = size // rows
        for slot, place in enumerate(places):
            weight_grads[place] = full[:, slot * high : (slot + 1) * high, :]

    def weight_sent(line, full, which):
        wait_bytes(full.at[pl.ds(0, rows - 1)], sems.at[2 * which])
        wait_bytes(line.at[pl.ds(0, cols - 1)], sems.at[2 * which + 2])
        wait_bytes(full.at[pl.ds(0, rows - 1)], sems.at[2 * which + 4])

    for part in range(PARTS):
        for_tiles(part, result_tile)
    put_weight(part_o, 0, dot_nt(norm_t[...], grad_o[...]))
    put_weight(part_o, 1, dot_nt(norm_s[...], grad_p[...]))
    weight_parts(part_o, held_o, WEIGHTS_O)
    for part in range(PARTS):
        arrived(GRADS, part)
        gather(recv_g, mat_g, part)
        for hop in hops:
            c = lax.rem(col + hop, cols)
            grads = dot_nn(strip_of(mat_g, part), spread[:, lanes(c)])
            send_strip(send_dl, recv_dl, LEFT_GRADS, part, hop, c, grads)
        keep_own(send_dl, recv_dl, part)
        if part == 0:
            weight_lines(held_o, line_o, WEIGHTS_O)

    def right_block(c, carry):
        outer = dot_tn(mat_g[:, lanes(c)], mat_l[...])
        for k in range(cols):
            block = outer[:, k * width : (k + 1) * width]
            block = block.reshape(2, per, 2, tiles, width)
            keep = jnp.where(low, block[0, :, 0], block[1, :, 1])
            turn = jnp.where(low, block[0, :, 1], block[1, :, 0])
            turn = pltpu.roll(turn.reshape(per * tiles, width), half_lanes, 1)
            total = (keep.reshape(per * tiles, width) + turn).reshape(
                per, PARTS, part_tiles, width
            )
            for part in range(PARTS):
                send_dr[part, k, pl.ds(c * per, per)] = total[:, part].astype(BF16)
        return carry

    lax.fori_loop(0, cols, right_block, 0)
    for part in range(PARTS):
        for_peers(lambda r, c: from_owner(send_dr, recv_dr, RIGHT_GRADS, part, r, c))
        keep_own(send_dr, recv_dr, part)
    weight_full(line_o, full_o, WEIGHTS_O)

    def edge_grads(p, q, value_ref, sig_ref):
        grad, sig = pad(p) * stage[strided(q), :], sig_ref[p]
        grad_v = grad * sig
        grad_e[:size, lanes(p)] = grad_v.astype(BF16)
        grad_e[size:, lanes(p)] = (grad_v * value_ref[p] * (1.0 - sig)).astype(BF16)

    def left_back(p, q):
        edge_grads(p, q, left_v, left_s)
        grad_n[p] += dot_nn(b_left[...], grad_e[:, lanes(p)])

    def right_back(p, q):
        edge_grads(p, q, right_v, right_s)

    def edge_weights(part):
        return dot_nt(norm_t[:, part_lanes(part)], grad_e[:, part_lanes(part)])

    def pair_tile(p, q):
        grad = grad_n[p] + dot_nn(b_right[...], grad_e[:, lanes(p)])
        hat = xhat[p]
        grad = scale[p] * (grad - mean_rows(grad) - hat * mean_rows(grad * hat))
        put_tile(grad_pair, p, grad)

    total = None
    for part in range(PARTS):
        arrived(LEFT_GRADS, part)
        unpack(recv_dl, part)
        for_tiles(part, left_back)
        both = edge_weights(part)
        total = both if part == 0 else total + both
    put_weight(part_l, 0, total[:, :size])
    put_weight(part_l, 1, total[:, size:])
    weight_parts(part_l, held_l, WEIGHTS_L)
    for part in range(PARTS):
        arrived(RIGHT_GRADS, part)
        unpack(recv_dr, part)
        for_tiles(part, right_back)
        both = edge_weights(part)
        total = both if part == 0 else total + both
        if part < PARTS - 1:
            for_tiles(part, pair_tile)
    put_weight(part_r, 0, total[:, :size])
    put_weight(part_r, 1, total[:, size:])
    weight_parts(part_r, held_r, WEIGHTS_R)
    weight_lines(held_l, line_l, WEIGHTS_L)
    weight_lines(held_r, line_r, WEIGHTS_R)
    for_tiles(PARTS - 1, pair_tile)
    weight_full(line_l, full_l, WEIGHTS_L)
    weight_store(full_o, WEIGHTS_O, (4, 5))
    weight_full(line_r, full_r, WEIGHTS_R)
    for which in range(6 * PARTS):
        sent(which)
    weight_sent(line_o, full_o, WEIGHTS_O)
    weight_store(full_l, WEIGHTS_L, (0, 1))
    weight_sent(line_l, full_l, WEIGHTS_L)
    weight_store(full_r, WEIGHTS_R, (2, 3))
    weight_sent(line_r, full_r, WEIGHTS_R)


def settle_kernel(count, *refs):
    arrays, outs, sems = refs[:count], refs[count : 2 * count], refs[-1]
    moves = [
        pltpu.make_async_copy(arrays[n], outs[n], sems.at[n]) for n in range(count)
    ]
    for move in moves:
        move.start()
    for move in moves:
        move.wait()


def settle(arrays):
    count = len(arrays)
    hbm = pl.BlockSpec(memory_space=pltpu.HBM)
    vmem = pl.BlockSpec(memory_space=pltpu.VMEM)
    return pl.pallas_call(
        functools.partial(settle_kernel, count),
        out_shape=tuple(jax.ShapeDtypeStruct(a.shape, a.dtype) for a in arrays),
        in_specs=[vmem] * count,
        out_specs=(hbm,) * count,
        scratch_shapes=[
            pltpu.SemaphoreType.DMA((count,)),
        ],
        compiler_params=pltpu.CompilerParams(vmem_limit_bytes=SETTLE_BYTES),
        name="settle",
    )(*arrays)


def shards(
    pair,
    pad_mask,
    crop_mask,
    left_proj,
    left_gate,
    right_proj,
    right_gate,
    out_gate,
    out_proj,
    cotangent,
):
    rows, cols = lax.axis_size("row"), lax.axis_size("col")
    high, wide, size = pair.shape
    tiles, width, channels = high // 2, 2 * wide, rows * cols
    positions = tiles * width
    hbm = pl.BlockSpec(memory_space=pltpu.HBM)
    vmem = pl.BlockSpec(memory_space=pltpu.VMEM)
    at_home = pltpu.VMEM((PARTS, channels, tiles // PARTS, width), BF16)
    at_owner = pltpu.VMEM((PARTS, cols, rows, tiles // PARTS, width), BF16)
    wide_tiles = pltpu.VMEM((tiles, size, width), F32)
    flat = pltpu.VMEM((size, positions), BF16)
    pair_weights = pltpu.VMEM((2 * size, size), BF16)
    weight = pltpu.VMEM((size, size), BF16)
    back_weights = pltpu.VMEM((size, 2 * size), BF16)
    share = size // rows

    def sum_buffers(count):
        return [
            pltpu.VMEM((rows, count * share, size), F32),
            pltpu.VMEM((rows, count * share, size), F32),
            pltpu.VMEM((cols, count * share, size), F32),
            pltpu.VMEM((rows, count * share, size), F32),
        ]

    outs = pl.pallas_call(
        functools.partial(kernel, rows, cols),
        out_shape=(
            pltpu.VMEM(pair.shape, BF16),
            pltpu.VMEM(pair.shape, BF16),
            pltpu.VMEM((6, rows, share, size), F32),
        ),
        in_specs=[hbm] * 10,
        out_specs=(vmem, vmem, vmem),
        scratch_shapes=[
            pltpu.VMEM(pair.shape, BF16),
            pltpu.VMEM(pair.shape, BF16),
            pltpu.SMEM(pad_mask.shape, jnp.int32),
            pltpu.SMEM(pad_mask.shape, jnp.int32),
            *[weight] * 6,
            pltpu.SemaphoreType.DMA((10,)),
            at_home,
            at_home,
            at_owner,
            at_home,
            at_owner,
            at_owner,
            at_owner,
            at_owner,
            at_home,
            at_owner,
            at_home,
            at_home,
            pltpu.VMEM((channels * tiles // PARTS, width), F32),
            pltpu.VMEM((cols * width, cols * width), BF16),
            pltpu.VMEM((rows * tiles, cols * width), BF16),
            pltpu.VMEM((rows * tiles, cols * width), BF16),
            flat,
            wide_tiles,
            pltpu.VMEM((tiles, 1, width), F32),
            wide_tiles,
            wide_tiles,
            wide_tiles,
            wide_tiles,
            wide_tiles,
            wide_tiles,
            wide_tiles,
            wide_tiles,
            flat,
            flat,
            flat,
            pltpu.VMEM((2 * size, positions), BF16),
            pair_weights,
            pair_weights,
            weight,
            weight,
            back_weights,
            back_weights,
            *sum_buffers(2) * 3,
            pltpu.SemaphoreType.DMA((2 * (WEIGHTS_R + 3),)),
        ],
        compiler_params=pltpu.CompilerParams(
            collective_id=1, has_side_effects=True, vmem_limit_bytes=VMEM_BYTES
        ),
        name="triangle",
    )(
        *[
            pltpu.with_memory_space_constraint(array, pltpu.HBM)
            for array in (
                pair,
                cotangent,
                pad_mask,
                crop_mask,
                left_proj,
                left_gate,
                right_proj,
                right_gate,
                out_gate,
                out_proj,
            )
        ]
    )
    result, grad_pair, weight_grads = settle(outs)
    return result, grad_pair, weight_grads.reshape(6, size, size)


def solution(mesh):
    blocks = P(("rep", "row"), "col", None)
    return jax.shard_map(
        shards,
        mesh=mesh,
        in_specs=(blocks, P("rep"), P("rep"), P(), P(), P(), P(), P(), P(), blocks),
        out_specs=(blocks, blocks, P("rep", None, None)),
        check_vma=False,
    )
```

```python
import functools

import jax
import jax.numpy as jnp
from jax import lax
from jax.experimental import pallas as pl
from jax.experimental.pallas import tpu as pltpu
from jax.sharding import PartitionSpec as P

MESH = pl.DeviceIdType.MESH
F32 = jnp.float32
BF16 = jnp.bfloat16
EPS = 1e-05
PARTS = 2
VMEM_BYTES = 50 * 2**20
SETTLE_BYTES = 4 * 2**20
LEFT, RIGHT, SUMS, GRADS, LEFT_GRADS, RIGHT_GRADS = (PARTS * n for n in range(6))
WEIGHTS_O, WEIGHTS_L, WEIGHTS_R = (6 * PARTS + 3 * n for n in range(3))


def dot_nn(left, right):
    return jnp.dot(left, right, preferred_element_type=F32)


def dot_nt(left, right):
    return lax.dot_general(left, right, (((1,), (1,)), ((), ())), preferred_element_type=F32)


def dot_tn(left, right):
    return lax.dot_general(left, right, (((0,), (0,)), ((), ())), preferred_element_type=F32)


def mean_rows(values):
    return jnp.mean(values, axis=0, keepdims=True)


def wait_bytes(ref, sem):
    pltpu.make_async_copy(ref, ref, sem).wait()


def kernel(
    rows,
    cols,
    pair_in,
    cot_in,
    pad_in,
    crop_in,
    left_proj_in,
    left_gate_in,
    right_proj_in,
    right_gate_in,
    out_gate_in,
    out_proj_in,
    result,
    grad_pair,
    weight_grads,
    pair,
    cot,
    pad_mask,
    crop_mask,
    left_proj,
    left_gate,
    right_proj,
    right_gate,
    out_gate,
    out_proj,
    in_sems,
    send_l,
    send_r,
    send_s,
    send_g,
    send_dl,
    send_dr,
    recv_l,
    recv_r,
    recv_s,
    recv_g,
    recv_dl,
    recv_dr,
    stage,
    spread,
    mat_l,
    mat_g,
    norm_t,
    xhat,
    scale,
    left_v,
    left_s,
    right_v,
    right_s,
    gate_c,
    gate_u,
    grad_ns,
    grad_n,
    norm_s,
    grad_p,
    grad_o,
    grad_e,
    w_left,
    w_right,
    w_out,
    w_proj,
    b_left,
    b_right,
    part_o,
    held_o,
    line_o,
    full_o,
    part_l,
    held_l,
    line_l,
    full_l,
    part_r,
    held_r,
    line_r,
    full_r,
    sems,
):
    row, col = lax.axis_index("row"), lax.axis_index("col")
    me = row * cols + col
    channels = rows * cols
    tiles, half_lanes = pair.shape[0] // 2, pair.shape[1]
    width, part_tiles, per = 2 * half_lanes, tiles // PARTS, rows // cols
    strip = rows * part_tiles
    order = sorted(range(cols), key=lambda step: min(step, cols - step))
    barrier = pltpu.get_barrier_semaphore()

    fetches = [
        pltpu.make_async_copy(source, target, in_sems.at[n])
        for n, (source, target) in enumerate(
            (
                (right_proj_in, right_proj),
                (right_gate_in, right_gate),
                (pad_in, pad_mask),
                (pair_in, pair),
                (left_proj_in, left_proj),
                (left_gate_in, left_gate),
                (crop_in, crop_mask),
                (out_gate_in, out_gate),
                (out_proj_in, out_proj),
                (cot_in, cot),
            )
        )
    ]
    for fetch in fetches:
        fetch.start()

    def device(r, c):
        return {"row": r, "col": c}

    def for_rows(act, itself):
        def step(shift, carry):
            act(lax.rem(row + shift, rows))
            return carry

        lax.fori_loop(0 if itself else 1, rows, step, 0)

    def for_peers(act):
        def step(shift, carry):
            for hop in order[:0:-1]:
                act(lax.rem(row + shift, rows), lax.rem(col + hop, cols))

            @pl.when(shift > 0)
            def _():
                act(lax.rem(row + shift, rows), col)

            return carry

        lax.fori_loop(0, rows, step, 0)

    for_peers(
        lambda r, c: pl.semaphore_signal(
            barrier, inc=1, device_id=device(r, c), device_id_type=MESH
        )
    )

    def copy_to(src, dst, which, r, c):
        pltpu.make_async_remote_copy(
            src_ref=src,
            dst_ref=dst,
            send_sem=sems.at[2 * which],
            recv_sem=sems.at[2 * which + 1],
            device_id=device(r, c),
            device_id_type=MESH,
        ).start()

    def to_owners(src, dst, which, part):
        dst[part, col, row] = src[part, me]
        for_peers(
            lambda r, c: copy_to(
                src.at[part, r * cols + c], dst.at[part, col, row], which + part, r, c
            )
        )

    def from_owner(src, dst, which, part, r, c):
        copy_to(src.at[part, c, r], dst.at[part, me], which + part, r, c)

    def keep_own(src, dst, part):
        dst[part, me] = src[part, col, row]

    def arrived(which, part):
        wait_bytes(send_l.at[0, pl.ds(0, channels - 1)], sems.at[2 * (which + part) + 1])

    def sent(which):
        wait_bytes(send_l.at[0, pl.ds(0, channels - 1)], sems.at[2 * which])

    def for_tiles(part, body):
        def step(q, carry):
            body(part * part_tiles + q, q)
            return carry

        lax.fori_loop(0, part_tiles, step, 0, unroll=8)

    def lanes(p):
        return pl.ds(pl.multiple_of(p * width, width), width)

    def strided(q):
        return pl.ds(q, channels, stride=part_tiles)

    def part_lanes(part):
        return pl.ds(part * part_tiles * width, part_tiles * width)

    def pack(dst, part):
        dst[part] = stage[...].reshape(channels, part_tiles, width).astype(BF16)

    def unpack(src, part):
        stage[...] = src[part].astype(F32).reshape(channels * part_tiles, width)

    lane = lax.broadcasted_iota(jnp.int32, (1, width), 1)
    low = lane < half_lanes

    def mask_of(ref):
        def put(n, line):
            value = ref[col * half_lanes + n].astype(F32)
            hit = jnp.logical_or(lane == n, lane == n + half_lanes)
            return jnp.where(hit, value, line)

        line = lax.fori_loop(0, half_lanes, put, jnp.zeros((1, width), F32), unroll=4)

        def mask(p):
            first = ref[row * 2 * tiles + p].astype(F32)
            second = ref[row * 2 * tiles + tiles + p].astype(F32)
            return jnp.where(low, first, second) * line

        return mask

    def tile_t(ref, p):
        both = jnp.concatenate([ref[p], ref[p + tiles]], axis=0)
        return both.astype(F32).T

    def put_tile(ref, p, values):
        back = values.T.astype(BF16)
        ref[p] = back[:half_lanes]
        ref[p + tiles] = back[half_lanes:]

    def flip(ref):
        return ref[...].astype(F32).T.astype(BF16)

    size = left_proj.shape[0]
    for fetch in fetches[:3]:
        fetch.wait()
    w_right[:size] = flip(right_proj)
    w_right[size:] = flip(right_gate)
    pad = mask_of(pad_mask)
    fetches[3].wait()

    def edge(p, q, normed, weight, value_ref, sig_ref):
        both = dot_nn(weight[...], normed)
        value, sig = both[:size], jax.nn.sigmoid(both[size:])
        value_ref[p] = value
        sig_ref[p] = sig
        stage[strided(q), :] = pad(p) * sig * value

    def right_tile(p, q):
        wide = tile_t(pair, p)
        center = wide - mean_rows(wide)
        rstd = lax.rsqrt(mean_rows(center * center) + EPS)
        hat = center * rstd
        xhat[p] = hat
        scale[p] = rstd
        normed = hat.astype(BF16)
        norm_t[:, lanes(p)] = normed
        edge(p, q, normed, w_right, right_v, right_s)

    def left_tile(p, q):
        edge(p, q, norm_t[:, lanes(p)], w_left, left_v, left_s)

    for part in range(PARTS):
        for_tiles(part, right_tile)
        pack(send_r, part)
        if part == 0:
            pl.semaphore_wait(barrier, channels - 1)
        to_owners(send_r, recv_r, RIGHT, part)
    for fetch in fetches[4:]:
        fetch.wait()
    w_left[:size] = flip(left_proj)
    w_left[size:] = flip(left_gate)
    for part in range(PARTS):
        for_tiles(part, left_tile)
        pack(send_l, part)
        to_owners(send_l, recv_l, LEFT, part)

    w_out[...] = flip(out_gate)
    w_proj[...] = flip(out_proj)
    b_left[:, :size] = left_proj[...]
    b_left[:, size:] = left_gate[...]
    b_right[:, :size] = right_proj[...]
    b_right[:, size:] = right_gate[...]
    crop = mask_of(crop_mask)

    def out_tile(p, q):
        gate = jax.nn.sigmoid(dot_nn(w_out[...], norm_t[:, lanes(p)]))
        upstream = crop(p) * tile_t(cot, p)
        projected_grad = (upstream * gate).astype(BF16)
        grad_p[:, lanes(p)] = projected_grad
        gate_c[p] = crop(p) * gate
        gate_u[p] = upstream * gate * (1.0 - gate)
        grad_ns[p] = dot_nn(out_proj[...], projected_grad)

    for part in range(PARTS):
        for_tiles(part, out_tile)

    for part in range(PARTS):
        arrived(RIGHT, part)

    def spread_block(k, carry):
        for c in range(cols):
            raw = recv_r[:, k, c * per : (c + 1) * per].astype(F32)
            turned = pltpu.roll(raw.reshape(PARTS * per * part_tiles, width), half_lanes, 1)
            turned = turned.reshape(raw.shape)
            pieces = []
            for half in range(2):
                for r in range(per):
                    for own in range(2):
                        for part in range(PARTS):
                            piece = raw[part, r] if half == own else turned[part, r]
                            keep = low if half == 0 else jnp.logical_not(low)
                            pieces.append(jnp.where(keep, piece, 0.0))
            block = jnp.concatenate(pieces, axis=0).astype(BF16)
            spread[c * width : (c + 1) * width, lanes(k)] = block
        return carry

    lax.fori_loop(0, cols, spread_block, 0)

    def gather(src, dst, part):
        for c in range(cols):
            block = src[part, c].astype(F32).reshape(strip, width).astype(BF16)
            dst[part * strip : (part + 1) * strip, c * width : (c + 1) * width] = block

    def send_strip(src, dst, which, part, hop, c, values):
        src[part, c] = values.reshape(rows, part_tiles, width).astype(BF16)
        for_rows(lambda r: from_owner(src, dst, which, part, r, c), hop != 0)

    def strip_of(mat, part):
        return mat[part * strip : (part + 1) * strip, :]

    hops = order[::-1]
    for part in range(PARTS):
        arrived(LEFT, part)
        gather(recv_l, mat_l, part)
        for hop in hops:
            c = lax.rem(col + hop, cols)
            sums = dot_nt(strip_of(mat_l, part), spread[lanes(c), :])
            send_strip(send_s, recv_s, SUMS, part, hop, c, sums)
        keep_own(send_s, recv_s, part)

    def sum_tile(p, q):
        sums = stage[strided(q), :]
        center = sums - mean_rows(sums)
        rstd = lax.rsqrt(mean_rows(center * center) + EPS)
        hat = center * rstd
        norm_s[:, lanes(p)] = hat.astype(BF16)
        grad = grad_ns[p]
        grad = rstd * (grad - mean_rows(grad) - hat * mean_rows(grad * hat))
        stage[strided(q), :] = grad

    for part in range(PARTS):
        arrived(SUMS, part)
        unpack(recv_s, part)
        for_tiles(part, sum_tile)
        pack(send_g, part)
        to_owners(send_g, recv_g, GRADS, part)

    def result_tile(p, q):
        projected = dot_nn(w_proj[...], norm_s[:, lanes(p)])
        put_tile(result, p, gate_c[p] * projected)
        logit = (gate_u[p] * projected).astype(BF16)
        grad_o[:, lanes(p)] = logit
        grad_n[p] = dot_nn(out_gate[...], logit)

    inverse = 1.0 / (rows * 2 * tiles)

    def put_weight(ref, place, values):
        high = size // rows
        ref[:, place * high : (place + 1) * high, :] = (values * inverse).reshape(
            rows, high, size
        )

    def weight_parts(part, held, which):
        held[row] = part[row]
        for_rows(lambda r: copy_to(part.at[r], held.at[row], which, r, col), False)

    def weight_lines(held, line, which):
        wait_bytes(held.at[pl.ds(0, rows - 1)], sems.at[2 * which + 1])
        line[col] = jnp.sum(held[...], axis=0)
        for hop in order[:0:-1]:
            copy_to(line.at[col], line.at[col], which + 1, row, lax.rem(col + hop, cols))

    def weight_full(line, full, which):
        wait_bytes(line.at[pl.ds(0, cols - 1)], sems.at[2 * which + 3])
        full[row] = jnp.sum(line[...], axis=0)
        for_rows(lambda r: copy_to(full.at[row], full.at[row], which + 2, r, col), False)

    def weight_store(full, which, places):
        wait_bytes(full.at[pl.ds(0, rows - 1)], sems.at[2 * which + 5])
        high = size // rows
        for slot, place in enumerate(places):
            weight_grads[place] = full[:, slot * high : (slot + 1) * high, :]

    def weight_sent(line, full, which):
        wait_bytes(full.at[pl.ds(0, rows - 1)], sems.at[2 * which])
        wait_bytes(line.at[pl.ds(0, cols - 1)], sems.at[2 * which + 2])
        wait_bytes(full.at[pl.ds(0, rows - 1)], sems.at[2 * which + 4])

    for part in range(PARTS):
        for_tiles(part, result_tile)
    put_weight(part_o, 0, dot_nt(norm_t[...], grad_o[...]))
    put_weight(part_o, 1, dot_nt(norm_s[...], grad_p[...]))
    weight_parts(part_o, held_o, WEIGHTS_O)
    for part in range(PARTS):
        arrived(GRADS, part)
        gather(recv_g, mat_g, part)
        for hop in hops:
            c = lax.rem(col + hop, cols)
            grads = dot_nn(strip_of(mat_g, part), spread[:, lanes(c)])
            send_strip(send_dl, recv_dl, LEFT_GRADS, part, hop, c, grads)
        keep_own(send_dl, recv_dl, part)
        if part == 0:
            weight_lines(held_o, line_o, WEIGHTS_O)

    def right_block(c, carry):
        outer = dot_tn(mat_g[:, lanes(c)], mat_l[...])
        for k in range(cols):
            block = outer[:, k * width : (k + 1) * width]
            block = block.reshape(2, per, 2, tiles, width)
            keep = jnp.where(low, block[0, :, 0], block[1, :, 1])
            turn = jnp.where(low, block[0, :, 1], block[1, :, 0])
            turn = pltpu.roll(turn.reshape(per * tiles, width), half_lanes, 1)
            total = (keep.reshape(per * tiles, width) + turn).reshape(
                per, PARTS, part_tiles, width
            )
            for part in range(PARTS):
                send_dr[part, k, pl.ds(c * per, per)] = total[:, part].astype(BF16)
        return carry

    lax.fori_loop(0, cols, right_block, 0)
    for part in range(PARTS):
        for_peers(lambda r, c: from_owner(send_dr, recv_dr, RIGHT_GRADS, part, r, c))
        keep_own(send_dr, recv_dr, part)
    weight_full(line_o, full_o, WEIGHTS_O)

    def edge_grads(p, q, value_ref, sig_ref):
        grad, sig = pad(p) * stage[strided(q), :], sig_ref[p]
        grad_v = grad * sig
        grad_e[:size, lanes(p)] = grad_v.astype(BF16)
        grad_e[size:, lanes(p)] = (grad_v * value_ref[p] * (1.0 - sig)).astype(BF16)

    def left_back(p, q):
        edge_grads(p, q, left_v, left_s)
        grad_n[p] += dot_nn(b_left[...], grad_e[:, lanes(p)])

    def right_back(p, q):
        edge_grads(p, q, right_v, right_s)

    def edge_weights(part):
        return dot_nt(norm_t[:, part_lanes(part)], grad_e[:, part_lanes(part)])

    def pair_tile(p, q):
        grad = grad_n[p] + dot_nn(b_right[...], grad_e[:, lanes(p)])
        hat = xhat[p]
        grad = scale[p] * (grad - mean_rows(grad) - hat * mean_rows(grad * hat))
        put_tile(grad_pair, p, grad)

    total = None
    for part in range(PARTS):
        arrived(LEFT_GRADS, part)
        unpack(recv_dl, part)
        for_tiles(part, left_back)
        both = edge_weights(part)
        total = both if part == 0 else total + both
    put_weight(part_l, 0, total[:, :size])
    put_weight(part_l, 1, total[:, size:])
    weight_parts(part_l, held_l, WEIGHTS_L)
    for part in range(PARTS):
        arrived(RIGHT_GRADS, part)
        unpack(recv_dr, part)
        for_tiles(part, right_back)
        both = edge_weights(part)
        total = both if part == 0 else total + both
        if part < PARTS - 1:
            for_tiles(part, pair_tile)
    put_weight(part_r, 0, total[:, :size])
    put_weight(part_r, 1, total[:, size:])
    weight_parts(part_r, held_r, WEIGHTS_R)
    weight_lines(held_l, line_l, WEIGHTS_L)
    weight_lines(held_r, line_r, WEIGHTS_R)
    for_tiles(PARTS - 1, pair_tile)
    weight_full(line_l, full_l, WEIGHTS_L)
    weight_store(full_o, WEIGHTS_O, (4, 5))
    weight_full(line_r, full_r, WEIGHTS_R)
    for which in range(6 * PARTS):
        sent(which)
    weight_sent(line_o, full_o, WEIGHTS_O)
    weight_store(full_l, WEIGHTS_L, (0, 1))
    weight_sent(line_l, full_l, WEIGHTS_L)
    weight_store(full_r, WEIGHTS_R, (2, 3))
    weight_sent(line_r, full_r, WEIGHTS_R)


def settle_kernel(count, *refs):
    arrays, outs, sems = refs[:count], refs[count : 2 * count], refs[-1]
    moves = [
        pltpu.make_async_copy(arrays[n], outs[n], sems.at[n]) for n in range(count)
    ]
    for move in moves:
        move.start()
    for move in moves:
        move.wait()


def settle(arrays):
    count = len(arrays)
    hbm = pl.BlockSpec(memory_space=pltpu.HBM)
    vmem = pl.BlockSpec(memory_space=pltpu.VMEM)
    return pl.pallas_call(
        functools.partial(settle_kernel, count),
        out_shape=tuple(jax.ShapeDtypeStruct(a.shape, a.dtype) for a in arrays),
        in_specs=[vmem] * count,
        out_specs=(hbm,) * count,
        scratch_shapes=[
            pltpu.SemaphoreType.DMA((count,)),
        ],
        compiler_params=pltpu.CompilerParams(vmem_limit_bytes=SETTLE_BYTES),
        name="settle",
    )(*arrays)


def shards(
    pair,
    pad_mask,
    crop_mask,
    left_proj,
    left_gate,
    right_proj,
    right_gate,
    out_gate,
    out_proj,
    cotangent,
):
    rows, cols = lax.axis_size("row"), lax.axis_size("col")
    high, wide, size = pair.shape
    tiles, width, channels = high // 2, 2 * wide, rows * cols
    positions = tiles * width
    hbm = pl.BlockSpec(memory_space=pltpu.HBM)
    vmem = pl.BlockSpec(memory_space=pltpu.VMEM)
    at_home = pltpu.VMEM((PARTS, channels, tiles // PARTS, width), BF16)
    at_owner = pltpu.VMEM((PARTS, cols, rows, tiles // PARTS, width), BF16)
    wide_tiles = pltpu.VMEM((tiles, size, width), F32)
    flat = pltpu.VMEM((size, positions), BF16)
    pair_weights = pltpu.VMEM((2 * size, size), BF16)
    weight = pltpu.VMEM((size, size), BF16)
    back_weights = pltpu.VMEM((size, 2 * size), BF16)
    share = size // rows

    def sum_buffers(count):
        return [
            pltpu.VMEM((rows, count * share, size), F32),
            pltpu.VMEM((rows, count * share, size), F32),
            pltpu.VMEM((cols, count * share, size), F32),
            pltpu.VMEM((rows, count * share, size), F32),
        ]

    outs = pl.pallas_call(
        functools.partial(kernel, rows, cols),
        out_shape=(
            pltpu.VMEM(pair.shape, BF16),
            pltpu.VMEM(pair.shape, BF16),
            pltpu.VMEM((6, rows, share, size), F32),
        ),
        in_specs=[hbm] * 10,
        out_specs=(vmem, vmem, vmem),
        scratch_shapes=[
            pltpu.VMEM(pair.shape, BF16),
            pltpu.VMEM(pair.shape, BF16),
            pltpu.SMEM(pad_mask.shape, jnp.int32),
            pltpu.SMEM(pad_mask.shape, jnp.int32),
            *[weight] * 6,
            pltpu.SemaphoreType.DMA((10,)),
            at_home,
            at_home,
            at_owner,
            at_home,
            at_owner,
            at_owner,
            at_owner,
            at_owner,
            at_home,
            at_owner,
            at_home,
            at_home,
            pltpu.VMEM((channels * tiles // PARTS, width), F32),
            pltpu.VMEM((cols * width, cols * width), BF16),
            pltpu.VMEM((rows * tiles, cols * width), BF16),
            pltpu.VMEM((rows * tiles, cols * width), BF16),
            flat,
            wide_tiles,
            pltpu.VMEM((tiles, 1, width), F32),
            wide_tiles,
            wide_tiles,
            wide_tiles,
            wide_tiles,
            wide_tiles,
            wide_tiles,
            wide_tiles,
            wide_tiles,
            flat,
            flat,
            flat,
            pltpu.VMEM((2 * size, positions), BF16),
            pair_weights,
            pair_weights,
            weight,
            weight,
            back_weights,
            back_weights,
            *sum_buffers(2) * 3,
            pltpu.SemaphoreType.DMA((2 * (WEIGHTS_R + 3),)),
        ],
        compiler_params=pltpu.CompilerParams(
            collective_id=1, has_side_effects=True, vmem_limit_bytes=VMEM_BYTES
        ),
        name="triangle",
    )(
        *[
            pltpu.with_memory_space_constraint(array, pltpu.HBM)
            for array in (
                pair,
                cotangent,
                pad_mask,
                crop_mask,
                left_proj,
                left_gate,
                right_proj,
                right_gate,
                out_gate,
                out_proj,
            )
        ]
    )
    result, grad_pair, weight_grads = settle(outs)
    return result, grad_pair, weight_grads.reshape(6, size, size)


def solution(mesh):
    blocks = P(("rep", "row"), "col", None)
    return jax.shard_map(
        shards,
        mesh=mesh,
        in_specs=(blocks, P("rep"), P("rep"), P(), P(), P(), P(), P(), P(), blocks),
        out_specs=(blocks, blocks, P("rep", None, None)),
        check_vma=False,
    )
```

```python
import functools

import jax
import jax.numpy as jnp
from jax import lax
from jax.experimental import pallas as pl
from jax.experimental.pallas import tpu as pltpu
from jax.sharding import PartitionSpec as P

MESH = pl.DeviceIdType.MESH
F32 = jnp.float32
BF16 = jnp.bfloat16
EPS = 1e-05
PARTS = 2
VMEM_BYTES = 50 * 2**20
SETTLE_BYTES = 4 * 2**20
LEFT, RIGHT, SUMS, GRADS, LEFT_GRADS, RIGHT_GRADS = (PARTS * n for n in range(6))
WEIGHTS_O, WEIGHTS_L, WEIGHTS_R = (6 * PARTS + 3 * n for n in range(3))


def dot_nn(left, right):
    return jnp.dot(left, right, preferred_element_type=F32)


def dot_nt(left, right):
    return lax.dot_general(left, right, (((1,), (1,)), ((), ())), preferred_element_type=F32)


def dot_tn(left, right):
    return lax.dot_general(left, right, (((0,), (0,)), ((), ())), preferred_element_type=F32)


def mean_rows(values):
    return jnp.mean(values, axis=0, keepdims=True)


def wait_bytes(ref, sem):
    pltpu.make_async_copy(ref, ref, sem).wait()


def kernel(
    rows,
    cols,
    pair_in,
    cot_in,
    pad_in,
    crop_in,
    left_proj_in,
    left_gate_in,
    right_proj_in,
    right_gate_in,
    out_gate_in,
    out_proj_in,
    result,
    grad_pair,
    weight_grads,
    pair,
    cot,
    pad_mask,
    crop_mask,
    left_proj,
    left_gate,
    right_proj,
    right_gate,
    out_gate,
    out_proj,
    in_sems,
    send_l,
    send_r,
    send_s,
    send_g,
    send_dl,
    send_dr,
    recv_l,
    recv_r,
    recv_s,
    recv_g,
    recv_dl,
    recv_dr,
    stage,
    spread,
    mat_l,
    mat_g,
    norm_t,
    xhat,
    scale,
    left_v,
    left_s,
    right_v,
    right_s,
    gate_c,
    gate_u,
    grad_ns,
    grad_n,
    norm_s,
    grad_p,
    grad_o,
    grad_e,
    w_left,
    w_right,
    w_out,
    w_proj,
    b_left,
    b_right,
    part_o,
    held_o,
    line_o,
    full_o,
    part_l,
    held_l,
    line_l,
    full_l,
    part_r,
    held_r,
    line_r,
    full_r,
    sems,
):
    row, col = lax.axis_index("row"), lax.axis_index("col")
    me = row * cols + col
    channels = rows * cols
    tiles, half_lanes = pair.shape[0] // 2, pair.shape[1]
    width, part_tiles, per = 2 * half_lanes, tiles // PARTS, rows // cols
    strip = rows * part_tiles
    order = sorted(range(cols), key=lambda step: min(step, cols - step))
    barrier = pltpu.get_barrier_semaphore()

    fetches = [
        pltpu.make_async_copy(source, target, in_sems.at[n])
        for n, (source, target) in enumerate(
            (
                (right_proj_in, right_proj),
                (right_gate_in, right_gate),
                (pad_in, pad_mask),
                (pair_in, pair),
                (left_proj_in, left_proj),
                (left_gate_in, left_gate),
                (crop_in, crop_mask),
                (out_gate_in, out_gate),
                (out_proj_in, out_proj),
                (cot_in, cot),
            )
        )
    ]
    for fetch in fetches:
        fetch.start()

    def device(r, c):
        return {"row": r, "col": c}

    def for_rows(act, itself):
        def step(shift, carry):
            act(lax.rem(row + shift, rows))
            return carry

        lax.fori_loop(0 if itself else 1, rows, step, 0)

    def for_peers(act):
        def step(shift, carry):
            for hop in order[:0:-1]:
                act(lax.rem(row + shift, rows), lax.rem(col + hop, cols))

            @pl.when(shift > 0)
            def _():
                act(lax.rem(row + shift, rows), col)

            return carry

        lax.fori_loop(0, rows, step, 0)

    for_peers(
        lambda r, c: pl.semaphore_signal(
            barrier, inc=1, device_id=device(r, c), device_id_type=MESH
        )
    )

    def copy_to(src, dst, which, r, c):
        pltpu.make_async_remote_copy(
            src_ref=src,
            dst_ref=dst,
            send_sem=sems.at[2 * which],
            recv_sem=sems.at[2 * which + 1],
            device_id=device(r, c),
            device_id_type=MESH,
        ).start()

    def to_owners(src, dst, which, part):
        dst[part, col, row] = src[part, me]
        for_peers(
            lambda r, c: copy_to(
                src.at[part, r * cols + c], dst.at[part, col, row], which + part, r, c
            )
        )

    def from_owner(src, dst, which, part, r, c):
        copy_to(src.at[part, c, r], dst.at[part, me], which + part, r, c)

    def keep_own(src, dst, part):
        dst[part, me] = src[part, col, row]

    def arrived(which, part):
        wait_bytes(send_l.at[0, pl.ds(0, channels - 1)], sems.at[2 * (which + part) + 1])

    def sent(which):
        wait_bytes(send_l.at[0, pl.ds(0, channels - 1)], sems.at[2 * which])

    def for_tiles(part, body):
        def step(q, carry):
            body(part * part_tiles + q, q)
            return carry

        lax.fori_loop(0, part_tiles, step, 0, unroll=8)

    def lanes(p):
        return pl.ds(pl.multiple_of(p * width, width), width)

    def strided(q):
        return pl.ds(q, channels, stride=part_tiles)

    def part_lanes(part):
        return pl.ds(part * part_tiles * width, part_tiles * width)

    def pack(dst, part):
        dst[part] = stage[...].reshape(channels, part_tiles, width).astype(BF16)

    def unpack(src, part):
        stage[...] = src[part].astype(F32).reshape(channels * part_tiles, width)

    lane = lax.broadcasted_iota(jnp.int32, (1, width), 1)
    low = lane < half_lanes

    def mask_of(ref):
        def put(n, line):
            value = ref[col * half_lanes + n].astype(F32)
            hit = jnp.logical_or(lane == n, lane == n + half_lanes)
            return jnp.where(hit, value, line)

        line = lax.fori_loop(0, half_lanes, put, jnp.zeros((1, width), F32), unroll=4)

        def mask(p):
            first = ref[row * 2 * tiles + p].astype(F32)
            second = ref[row * 2 * tiles + tiles + p].astype(F32)
            return jnp.where(low, first, second) * line

        return mask

    def tile_t(ref, p):
        both = jnp.concatenate([ref[p], ref[p + tiles]], axis=0)
        return both.astype(F32).T

    def put_tile(ref, p, values):
        back = values.T.astype(BF16)
        ref[p] = back[:half_lanes]
        ref[p + tiles] = back[half_lanes:]

    def flip(ref):
        return ref[...].astype(F32).T.astype(BF16)

    size = left_proj.shape[0]
    for fetch in fetches[:3]:
        fetch.wait()
    w_right[:size] = flip(right_proj)
    w_right[size:] = flip(right_gate)
    pad = mask_of(pad_mask)
    fetches[3].wait()

    def edge(p, q, normed, weight, value_ref, sig_ref):
        both = dot_nn(weight[...], normed)
        value, sig = both[:size], jax.nn.sigmoid(both[size:])
        value_ref[p] = value
        sig_ref[p] = sig
        stage[strided(q), :] = pad(p) * sig * value

    def right_tile(p, q):
        wide = tile_t(pair, p)
        center = wide - mean_rows(wide)
        rstd = lax.rsqrt(mean_rows(center * center) + EPS)
        hat = center * rstd
        xhat[p] = hat
        scale[p] = rstd
        normed = hat.astype(BF16)
        norm_t[:, lanes(p)] = normed
        edge(p, q, normed, w_right, right_v, right_s)

    def left_tile(p, q):
        edge(p, q, norm_t[:, lanes(p)], w_left, left_v, left_s)

    for part in range(PARTS):
        for_tiles(part, right_tile)
        pack(send_r, part)
        if part == 0:
            pl.semaphore_wait(barrier, channels - 1)
        to_owners(send_r, recv_r, RIGHT, part)
    for fetch in fetches[4:]:
        fetch.wait()
    w_left[:size] = flip(left_proj)
    w_left[size:] = flip(left_gate)
    for part in range(PARTS):
        for_tiles(part, left_tile)
        pack(send_l, part)
        to_owners(send_l, recv_l, LEFT, part)

    w_out[...] = flip(out_gate)
    w_proj[...] = flip(out_proj)
    b_left[:, :size] = left_proj[...]
    b_left[:, size:] = left_gate[...]
    b_right[:, :size] = right_proj[...]
    b_right[:, size:] = right_gate[...]
    crop = mask_of(crop_mask)

    def out_tile(p, q):
        gate = jax.nn.sigmoid(dot_nn(w_out[...], norm_t[:, lanes(p)]))
        upstream = crop(p) * tile_t(cot, p)
        projected_grad = (upstream * gate).astype(BF16)
        grad_p[:, lanes(p)] = projected_grad
        gate_c[p] = crop(p) * gate
        gate_u[p] = upstream * gate * (1.0 - gate)
        back = dot_nn(out_proj[...], projected_grad)
        grad_ns[p] = back - mean_rows(back)
        for value_ref, sig_ref in ((left_v, left_s), (right_v, right_s)):
            sig = sig_ref[p]
            slope = pad(p) * sig
            value_ref[p] = slope * value_ref[p] * (1.0 - sig)
            sig_ref[p] = slope

    for part in range(PARTS):
        for_tiles(part, out_tile)

    for part in range(PARTS):
        arrived(RIGHT, part)

    def spread_block(k, carry):
        for c in range(cols):
            raw = recv_r[:, k, c * per : (c + 1) * per].astype(F32)
            turned = pltpu.roll(raw.reshape(PARTS * per * part_tiles, width), half_lanes, 1)
            turned = turned.reshape(raw.shape)
            pieces = []
            for half in range(2):
                for r in range(per):
                    for own in range(2):
                        for part in range(PARTS):
                            piece = raw[part, r] if half == own else turned[part, r]
                            keep = low if half == 0 else jnp.logical_not(low)
                            pieces.append(jnp.where(keep, piece, 0.0))
            block = jnp.concatenate(pieces, axis=0).astype(BF16)
            spread[c * width : (c + 1) * width, lanes(k)] = block
        return carry

    lax.fori_loop(0, cols, spread_block, 0)

    def gather(src, dst, part):
        for c in range(cols):
            block = src[part, c].astype(F32).reshape(strip, width).astype(BF16)
            dst[part * strip : (part + 1) * strip, c * width : (c + 1) * width] = block

    def send_strip(src, dst, which, part, hop, c, values):
        src[part, c] = values.reshape(rows, part_tiles, width).astype(BF16)
        for_rows(lambda r: from_owner(src, dst, which, part, r, c), hop != 0)

    def strip_of(mat, part):
        return mat[part * strip : (part + 1) * strip, :]

    hops = order[::-1]
    for part in range(PARTS):
        arrived(LEFT, part)
        gather(recv_l, mat_l, part)
        for hop in hops:
            c = lax.rem(col + hop, cols)
            sums = dot_nt(strip_of(mat_l, part), spread[lanes(c), :])
            send_strip(send_s, recv_s, SUMS, part, hop, c, sums)
        keep_own(send_s, recv_s, part)

    def sum_tile(p, q):
        sums = stage[strided(q), :]
        center = sums - mean_rows(sums)
        rstd = lax.rsqrt(mean_rows(center * center) + EPS)
        hat = center * rstd
        norm_s[:, lanes(p)] = hat.astype(BF16)
        grad = grad_ns[p]
        grad = rstd * (grad - hat * mean_rows(grad * hat))
        stage[strided(q), :] = grad

    for part in range(PARTS):
        arrived(SUMS, part)
        unpack(recv_s, part)
        for_tiles(part, sum_tile)
        pack(send_g, part)
        to_owners(send_g, recv_g, GRADS, part)

    def result_tile(p, q):
        projected = dot_nn(w_proj[...], norm_s[:, lanes(p)])
        put_tile(result, p, gate_c[p] * projected)
        logit = (gate_u[p] * projected).astype(BF16)
        grad_o[:, lanes(p)] = logit
        grad_n[p] = dot_nn(out_gate[...], logit)

    inverse = 1.0 / (rows * 2 * tiles)

    def put_weight(ref, place, values):
        high = size // rows
        ref[:, place * high : (place + 1) * high, :] = (values * inverse).reshape(
            rows, high, size
        )

    def weight_parts(part, held, which):
        held[row] = part[row]
        for_rows(lambda r: copy_to(part.at[r], held.at[row], which, r, col), False)

    def weight_lines(held, line, which):
        wait_bytes(held.at[pl.ds(0, rows - 1)], sems.at[2 * which + 1])
        line[col] = jnp.sum(held[...], axis=0)
        for hop in order[:0:-1]:
            copy_to(line.at[col], line.at[col], which + 1, row, lax.rem(col + hop, cols))

    def weight_full(line, full, which):
        wait_bytes(line.at[pl.ds(0, cols - 1)], sems.at[2 * which + 3])
        full[row] = jnp.sum(line[...], axis=0)
        for_rows(lambda r: copy_to(full.at[row], full.at[row], which + 2, r, col), False)

    def weight_store(full, which, places):
        wait_bytes(full.at[pl.ds(0, rows - 1)], sems.at[2 * which + 5])
        high = size // rows
        for slot, place in enumerate(places):
            weight_grads[place] = full[:, slot * high : (slot + 1) * high, :]

    def weight_sent(line, full, which):
        wait_bytes(full.at[pl.ds(0, rows - 1)], sems.at[2 * which])
        wait_bytes(line.at[pl.ds(0, cols - 1)], sems.at[2 * which + 2])
        wait_bytes(full.at[pl.ds(0, rows - 1)], sems.at[2 * which + 4])

    for part in range(PARTS):
        for_tiles(part, result_tile)
    put_weight(part_o, 0, dot_nt(norm_t[...], grad_o[...]))
    put_weight(part_o, 1, dot_nt(norm_s[...], grad_p[...]))
    weight_parts(part_o, held_o, WEIGHTS_O)
    for part in range(PARTS):
        arrived(GRADS, part)
        gather(recv_g, mat_g, part)
        for hop in hops:
            c = lax.rem(col + hop, cols)
            grads = dot_nn(strip_of(mat_g, part), spread[:, lanes(c)])
            send_strip(send_dl, recv_dl, LEFT_GRADS, part, hop, c, grads)
        keep_own(send_dl, recv_dl, part)
        if part == 0:
            weight_lines(held_o, line_o, WEIGHTS_O)

    def right_block(c, carry):
        outer = dot_tn(mat_g[:, lanes(c)], mat_l[...])
        for k in range(cols):
            block = outer[:, k * width : (k + 1) * width]
            block = block.reshape(2, per, 2, tiles, width)
            keep = jnp.where(low, block[0, :, 0], block[1, :, 1])
            turn = jnp.where(low, block[0, :, 1], block[1, :, 0])
            turn = pltpu.roll(turn.reshape(per * tiles, width), half_lanes, 1)
            total = (keep.reshape(per * tiles, width) + turn).reshape(
                per, PARTS, part_tiles, width
            )
            for part in range(PARTS):
                send_dr[part, k, pl.ds(c * per, per)] = total[:, part].astype(BF16)
        return carry

    lax.fori_loop(0, cols, right_block, 0)
    for part in range(PARTS):
        for_peers(lambda r, c: from_owner(send_dr, recv_dr, RIGHT_GRADS, part, r, c))
        keep_own(send_dr, recv_dr, part)
    weight_full(line_o, full_o, WEIGHTS_O)

    def edge_grads(p, q, value_ref, sig_ref):
        grad = stage[strided(q), :]
        grad_e[:size, lanes(p)] = (grad * sig_ref[p]).astype(BF16)
        grad_e[size:, lanes(p)] = (grad * value_ref[p]).astype(BF16)

    def left_back(p, q):
        edge_grads(p, q, left_v, left_s)
        grad_n[p] += dot_nn(b_left[...], grad_e[:, lanes(p)])

    def right_back(p, q):
        edge_grads(p, q, right_v, right_s)

    def edge_weights(part):
        return dot_nt(norm_t[:, part_lanes(part)], grad_e[:, part_lanes(part)])

    def pair_tile(p, q):
        grad = grad_n[p] + dot_nn(b_right[...], grad_e[:, lanes(p)])
        hat = xhat[p]
        grad = scale[p] * (grad - mean_rows(grad) - hat * mean_rows(grad * hat))
        put_tile(grad_pair, p, grad)

    total = None
    for part in range(PARTS):
        arrived(LEFT_GRADS, part)
        unpack(recv_dl, part)
        for_tiles(part, left_back)
        both = edge_weights(part)
        total = both if part == 0 else total + both
    put_weight(part_l, 0, total[:, :size])
    put_weight(part_l, 1, total[:, size:])
    weight_parts(part_l, held_l, WEIGHTS_L)
    for part in range(PARTS):
        arrived(RIGHT_GRADS, part)
        unpack(recv_dr, part)
        for_tiles(part, right_back)
        both = edge_weights(part)
        total = both if part == 0 else total + both
        if part < PARTS - 1:
            for_tiles(part, pair_tile)
    put_weight(part_r, 0, total[:, :size])
    put_weight(part_r, 1, total[:, size:])
    weight_parts(part_r, held_r, WEIGHTS_R)
    weight_lines(held_l, line_l, WEIGHTS_L)
    weight_lines(held_r, line_r, WEIGHTS_R)
    for_tiles(PARTS - 1, pair_tile)
    weight_full(line_l, full_l, WEIGHTS_L)
    weight_store(full_o, WEIGHTS_O, (4, 5))
    weight_full(line_r, full_r, WEIGHTS_R)
    for which in range(6 * PARTS):
        sent(which)
    weight_sent(line_o, full_o, WEIGHTS_O)
    weight_store(full_l, WEIGHTS_L, (0, 1))
    weight_sent(line_l, full_l, WEIGHTS_L)
    weight_store(full_r, WEIGHTS_R, (2, 3))
    weight_sent(line_r, full_r, WEIGHTS_R)


def settle_kernel(count, *refs):
    arrays, outs, sems = refs[:count], refs[count : 2 * count], refs[-1]
    moves = [
        pltpu.make_async_copy(arrays[n], outs[n], sems.at[n]) for n in range(count)
    ]
    for move in moves:
        move.start()
    for move in moves:
        move.wait()


def settle(arrays):
    count = len(arrays)
    hbm = pl.BlockSpec(memory_space=pltpu.HBM)
    vmem = pl.BlockSpec(memory_space=pltpu.VMEM)
    return pl.pallas_call(
        functools.partial(settle_kernel, count),
        out_shape=tuple(jax.ShapeDtypeStruct(a.shape, a.dtype) for a in arrays),
        in_specs=[vmem] * count,
        out_specs=(hbm,) * count,
        scratch_shapes=[
            pltpu.SemaphoreType.DMA((count,)),
        ],
        compiler_params=pltpu.CompilerParams(vmem_limit_bytes=SETTLE_BYTES),
        name="settle",
    )(*arrays)


def shards(
    pair,
    pad_mask,
    crop_mask,
    left_proj,
    left_gate,
    right_proj,
    right_gate,
    out_gate,
    out_proj,
    cotangent,
):
    rows, cols = lax.axis_size("row"), lax.axis_size("col")
    high, wide, size = pair.shape
    tiles, width, channels = high // 2, 2 * wide, rows * cols
    positions = tiles * width
    hbm = pl.BlockSpec(memory_space=pltpu.HBM)
    vmem = pl.BlockSpec(memory_space=pltpu.VMEM)
    at_home = pltpu.VMEM((PARTS, channels, tiles // PARTS, width), BF16)
    at_owner = pltpu.VMEM((PARTS, cols, rows, tiles // PARTS, width), BF16)
    wide_tiles = pltpu.VMEM((tiles, size, width), F32)
    flat = pltpu.VMEM((size, positions), BF16)
    pair_weights = pltpu.VMEM((2 * size, size), BF16)
    weight = pltpu.VMEM((size, size), BF16)
    back_weights = pltpu.VMEM((size, 2 * size), BF16)
    share = size // rows

    def sum_buffers(count):
        return [
            pltpu.VMEM((rows, count * share, size), F32),
            pltpu.VMEM((rows, count * share, size), F32),
            pltpu.VMEM((cols, count * share, size), F32),
            pltpu.VMEM((rows, count * share, size), F32),
        ]

    outs = pl.pallas_call(
        functools.partial(kernel, rows, cols),
        out_shape=(
            pltpu.VMEM(pair.shape, BF16),
            pltpu.VMEM(pair.shape, BF16),
            pltpu.VMEM((6, rows, share, size), F32),
        ),
        in_specs=[hbm] * 10,
        out_specs=(vmem, vmem, vmem),
        scratch_shapes=[
            pltpu.VMEM(pair.shape, BF16),
            pltpu.VMEM(pair.shape, BF16),
            pltpu.SMEM(pad_mask.shape, jnp.int32),
            pltpu.SMEM(pad_mask.shape, jnp.int32),
            *[weight] * 6,
            pltpu.SemaphoreType.DMA((10,)),
            at_home,
            at_home,
            at_owner,
            at_home,
            at_owner,
            at_owner,
            at_owner,
            at_owner,
            at_home,
            at_owner,
            at_home,
            at_home,
            pltpu.VMEM((channels * tiles // PARTS, width), F32),
            pltpu.VMEM((cols * width, cols * width), BF16),
            pltpu.VMEM((rows * tiles, cols * width), BF16),
            pltpu.VMEM((rows * tiles, cols * width), BF16),
            flat,
            wide_tiles,
            pltpu.VMEM((tiles, 1, width), F32),
            wide_tiles,
            wide_tiles,
            wide_tiles,
            wide_tiles,
            wide_tiles,
            wide_tiles,
            wide_tiles,
            wide_tiles,
            flat,
            flat,
            flat,
            pltpu.VMEM((2 * size, positions), BF16),
            pair_weights,
            pair_weights,
            weight,
            weight,
            back_weights,
            back_weights,
            *sum_buffers(2) * 3,
            pltpu.SemaphoreType.DMA((2 * (WEIGHTS_R + 3),)),
        ],
        compiler_params=pltpu.CompilerParams(
            collective_id=1, has_side_effects=True, vmem_limit_bytes=VMEM_BYTES
        ),
        name="triangle",
    )(
        *[
            pltpu.with_memory_space_constraint(array, pltpu.HBM)
            for array in (
                pair,
                cotangent,
                pad_mask,
                crop_mask,
                left_proj,
                left_gate,
                right_proj,
                right_gate,
                out_gate,
                out_proj,
            )
        ]
    )
    result, grad_pair, weight_grads = settle(outs)
    return result, grad_pair, weight_grads.reshape(6, size, size)


def solution(mesh):
    blocks = P(("rep", "row"), "col", None)
    return jax.shard_map(
        shards,
        mesh=mesh,
        in_specs=(blocks, P("rep"), P("rep"), P(), P(), P(), P(), P(), P(), blocks),
        out_specs=(blocks, blocks, P("rep", None, None)),
        check_vma=False,
    )
```
